32 devices in a mesh: ha: 8 (over y, x, core), wa: 4 (over z).
Axes of the slice: x: 2, y: 2, z: 4, core: 2. Of those that a mesh axis runs over, the one named last changes fastest.
Arguments:
- frames: bfloat16 [2, 128, 256, 384], P(None, 'ha', 'wa'), may hold values from -6 to 6
- keep: int32 [2, 3], replicated, may hold values 0 or 1
- expand_weight: bfloat16 [384, 1536], replicated, may hold values from -0.3125 to 0.3125
- dw_kernel: float32 [3, 3, 1536], replicated, may hold values from -2 to 2
- conv_bias: float32 [1536], replicated, may hold values from -3 to 3
- project_weight: bfloat16 [1536, 384], replicated, may hold values from -0.15625 to 0.15625
- qkv_weight: bfloat16 [384, 1152], replicated, may hold values from -4 to 4
- out_weight: bfloat16 [384, 384], replicated, may hold values from -0.3125 to 0.3125
- mlp_in: bfloat16 [384, 1536], replicated, may hold values from -0.3125 to 0.3125
- mlp_out: bfloat16 [1536, 384], replicated, may hold values from -0.15625 to 0.15625
Outputs:
- result: bfloat16 [2, 128, 256, 384], P(None, 'ha', 'wa')
The draws below stay inside these ranges and needn't reach their ends.
All inputs are finite; a program needn't handle non-finite values.
Results may differ from the reference program's by a relative error of at most 0.0068.
Values may be sent and summed in bfloat16 or wider, within the bound.
No kernel may reach another device: no remote copies, remote signals or barrier semaphores. Data moves between devices by JAX's collectives and lax.ppermute only.
A program may use at most 64 MiB of HBM per device.

```python
import math
import jax
import jax.numpy as jnp
from jax import lax

C = 384
EXP = 1536
HEADS = 12
FFN = 1536
GRID = 16
FRAMES = 2
H = 128
W = 256


def draw_qkv_weight(key, part):
    first_key = jax.random.fold_in(key, 0)
    whole = jax.random.normal(first_key, (C, 3 * C), jnp.float32) / math.sqrt(C)
    return jnp.clip(whole, -4.0, 4.0).astype(jnp.bfloat16)


def place_ends(array, stream_key, smallest, top_value):
    extent = array.shape
    spot = [jax.random.randint(jax.random.fold_in(stream_key, axis), (), 0, extent[axis]) for axis in range(len(extent))]
    array = array.at[tuple(spot)].set(smallest)
    longest = extent.index(max(extent))
    spot[longest] = (spot[longest] + 1) % extent[longest]
    return array.at[tuple(spot)].set(top_value)


def levels(stream_key, dims, shards, smallest, high):
    def one(axis_at, shards_of):
        draws = jax.random.uniform(jax.random.fold_in(jax.random.fold_in(stream_key, 6), axis_at), (shards_of,), jnp.float32, smallest / len(shards), high / len(shards))
        return jnp.repeat(jnp.exp(draws), dims[axis_at] // shards_of).reshape((-1,) + (1,) * (len(dims) - axis_at - 1))

    loudness = one(*shards[0])
    for cut in shards[1:]:
        loudness = loudness * one(*cut)
    return loudness


def normal_values(stream_key, extent, scale, limit, shards=(), kind=jnp.bfloat16):
    array = jax.random.normal(stream_key, extent, jnp.float32) * scale
    if len(shards) > 0:
        array = levels(stream_key, extent, shards, -0.22, 0.18) * array
    return jnp.clip(array, min=-limit, max=limit).astype(kind)


def setup_inputs(seed: int = 0) -> dict:
    key_of = jax.random.split(jax.random.key(seed), 11)
    return {
        "frames": normal_values(key_of[0], (FRAMES, H, W, C), 1.0, 6.0, ((1, 8), (2, 4))),
        "keep": place_ends((jax.random.randint(key_of[1], (FRAMES, 3), 0, 5) < 4).astype(jnp.int32), jax.random.fold_in(key_of[1], 1), 0, 1),
        "expand_weight": normal_values(key_of[2], (C, EXP), C ** -0.5, 0.3125),
        "dw_kernel": normal_values(key_of[3], (3, 3, EXP), 0.33, 2.0, (), jnp.float32),
        "conv_bias": normal_values(key_of[4], (EXP,), 0.5, 3.0, (), jnp.float32),
        "project_weight": normal_values(key_of[5], (EXP, C), EXP ** -0.5, 0.15625),
        "qkv_weight": draw_qkv_weight(jax.random.fold_in(key_of[10], 71), 0),
        "out_weight": normal_values(key_of[7], (C, C), C ** -0.5, 0.3125),
        "mlp_in": normal_values(key_of[8], (C, FFN), C ** -0.5, 0.3125),
        "mlp_out": normal_values(key_of[9], (FFN, C), FFN ** -0.5, 0.15625),
    }


def normalize(values):
    mean_val = lax.optimization_barrier(jnp.mean(values, axis=-1, keepdims=True))
    centred = values - mean_val
    variance = lax.optimization_barrier(jnp.mean(centred * centred, axis=-1, keepdims=True))
    return centred * lax.rsqrt(variance + 1e-05)

def conv_branch(padded_in, dw_kernel, conv_bias, expand_weight, project_weight):
    row_count = padded_in.shape[0] - 2
    col_count = padded_in.shape[1] - 2
    expanded = jax.nn.gelu(jnp.dot(padded_in, expand_weight, preferred_element_type=jnp.float32)).astype(jnp.bfloat16)
    total = jnp.zeros((row_count, col_count, expanded.shape[-1]), jnp.float32)
    for shift_y in range(3):
        for shift_x in range(3):
            total = total + expanded[shift_y:shift_y + row_count, shift_x:shift_x + col_count].astype(jnp.float32) * dw_kernel[shift_y, shift_x]
    mixed = jax.nn.gelu(total + conv_bias).astype(jnp.bfloat16)
    return jnp.dot(mixed, project_weight, preferred_element_type=jnp.float32)

def attend(block, window_flag, qkv_weight, out_weight):
    pair_count, token_count, channels = block.shape
    head_dim = channels // HEADS
    residual = block.astype(jnp.float32)
    normed = normalize(residual).astype(jnp.bfloat16)
    qkv = jnp.dot(normed, qkv_weight, preferred_element_type=jnp.float32).astype(jnp.bfloat16)
    queries = qkv[..., :channels].reshape(pair_count, token_count, HEADS, head_dim).astype(jnp.float32)
    keys_part = qkv[..., channels:2 * channels].reshape(pair_count, token_count, HEADS, head_dim).astype(jnp.float32)
    values_part = qkv[..., 2 * channels:].reshape(pair_count, token_count, HEADS, head_dim).astype(jnp.float32)
    scores = jnp.einsum('bqhd,bkhd->bhqk', queries, keys_part) * head_dim ** (-0.5)
    top_score = lax.optimization_barrier(jnp.max(scores, axis=-1, keepdims=True))
    weights = jnp.exp(scores - top_score)
    probs = (weights / lax.optimization_barrier(jnp.sum(weights, axis=-1, keepdims=True))).astype(jnp.bfloat16)
    attended = jnp.einsum('bhqk,bkhd->bqhd', probs.astype(jnp.float32), values_part)
    attended = attended.astype(jnp.bfloat16).reshape(pair_count, token_count, channels)
    update = jnp.dot(attended, out_weight, preferred_element_type=jnp.float32)
    return (residual + window_flag[:, None, None] * update).astype(jnp.bfloat16)

def mlp_piece(piece, flag, mlp_in, mlp_out):
    residual = piece.astype(jnp.float32)
    normed = normalize(residual).astype(jnp.bfloat16)
    inner = jax.nn.gelu(jnp.dot(normed, mlp_in, preferred_element_type=jnp.float32)).astype(jnp.bfloat16)
    return (residual + flag * jnp.dot(inner, mlp_out, preferred_element_type=jnp.float32)).astype(jnp.bfloat16)

def reference(frames, keep, expand_weight, dw_kernel, conv_bias, project_weight, qkv_weight, out_weight, mlp_in, mlp_out):
    flags = keep.astype(jnp.float32)
    block_rows = 16
    section_one = []
    for frame in range(FRAMES):
        padded = jnp.pad(frames[frame], ((1, 1), (1, 1), (0, 0)))

        def one_block(index):
            start = (index * block_rows).astype(jnp.int32)
            piece = lax.dynamic_slice_in_dim(padded, start, block_rows + 2, 0)
            return conv_branch(piece, dw_kernel, conv_bias, expand_weight, project_weight)
        branch = lax.map(one_block, jnp.arange(H // block_rows, dtype=jnp.int32)).reshape(H, W, C)
        section_one.append((frames[frame].astype(jnp.float32) + flags[frame, 0] * branch).astype(jnp.bfloat16))
    first = jnp.stack(section_one)
    windows = first.reshape(FRAMES, GRID, H // GRID, GRID, W // GRID, C).transpose(0, 2, 4, 1, 3, 5)
    windows = windows.reshape(-1, GRID * GRID, C)
    window_count = windows.shape[0]
    window_flags = jnp.repeat(flags[:, 1], window_count // FRAMES).reshape(window_count // 2, 2)
    blocks = windows.reshape(window_count // 2, 2, GRID * GRID, C)

    def one_pair(pair):
        return attend(pair[0], pair[1], qkv_weight, out_weight)
    second = lax.map(one_pair, (blocks, window_flags))
    second = second.reshape(FRAMES, H // GRID, W // GRID, GRID, GRID, C).transpose(0, 3, 1, 4, 2, 5).reshape(FRAMES, H, W, C)
    outputs = []
    for frame in range(FRAMES):
        pieces = second[frame].reshape(H // block_rows, block_rows, W, C)
        frame_flag = flags[frame, 2]

        def one_piece(piece):
            return mlp_piece(piece, frame_flag, mlp_in, mlp_out)
        outputs.append(lax.map(one_piece, pieces).reshape(H, W, C))
    return jnp.stack(outputs)
```

```python
import math

import jax
import jax.numpy as jnp
import numpy as np
from jax import lax
from jax.experimental import pallas as pl
from jax.experimental.pallas import tpu as pltpu
from jax.sharding import PartitionSpec as P

HEADS = 12
GRID = 16
SEG = 8
CHUNK = 256
F32 = jnp.float32
BF16 = jnp.bfloat16
VMEM_LIMIT = 40 * 1024 * 1024


def gelu(v):
    cubic = v * (math.sqrt(2 / math.pi) + (math.sqrt(2 / math.pi) * 0.044715) * (v * v))
    half = 0.5 * v
    return half + half * jnp.tanh(cubic)


def normalize(values):
    mean_val = jnp.mean(values, axis=-1, keepdims=True)
    centred = values - mean_val
    variance = jnp.mean(centred * centred, axis=-1, keepdims=True)
    return centred * lax.rsqrt(variance + 1e-05)


def dot(a, b):
    return jnp.dot(a, b, preferred_element_type=F32)


def dot_t(a, b):
    return lax.dot_general(a, b, (((1,), (1,)), ((), ())), preferred_element_type=F32)


def segment_order(cols, count):
    steps = cols // SEG
    matrix = np.zeros((count * cols, count * cols), np.float32)
    for row in range(count):
        for t in range(steps):
            for s in range(SEG):
                matrix[row * cols + t * SEG + s, row * cols + s * steps + t] = 1
    return matrix


def message_order(row_groups, cols, col_stride, cols_each):
    col_groups = cols // col_stride
    dests = col_stride // cols_each
    matrix = np.zeros((row_groups * cols, row_groups * cols), np.float32)
    place = 0
    for w in range(dests):
        for b in range(cols_each):
            for g in range(row_groups):
                for h in range(col_groups):
                    matrix[place, g * cols + h * col_stride + w * cols_each + b] = 1
                    place += 1
    return matrix


def conv_kernel(
    frame,
    keep_ref,
    x_ref,
    top_ref,
    bottom_ref,
    left_ref,
    right_ref,
    seg_ref,
    order_ref,
    expand_ref,
    dw_ref,
    bias_ref,
    project_ref,
    out_ref,
    tokens,
    sides,
    side_vals,
    expanded,
    mixed,
    total,
):
    step = pl.program_id(0)
    rows, cols, channels = x_ref.shape
    steps = cols // SEG
    width = expand_ref.shape[1]

    @pl.when(step == 0)
    def _():
        pair = 2 * cols
        seg_pair = seg_ref[...]
        seg_one = seg_pair[:cols, :cols]
        tokens[0:cols] = dot(seg_one, top_ref[0:cols]).astype(BF16)
        for r in range(rows // 2):
            both = x_ref[2 * r : 2 * r + 2].reshape(pair, channels)
            tokens[cols + r * pair : cols + (r + 1) * pair] = dot(seg_pair, both).astype(BF16)
        tokens[(rows + 1) * cols : (rows + 2) * cols] = dot(seg_one, bottom_ref[0:cols]).astype(BF16)
        sides[...] = jnp.zeros_like(sides)
        top = top_ref[cols : cols + 16].astype(F32)
        bottom = bottom_ref[cols : cols + 16].astype(F32)
        sides[0:1] = top[0:1]
        sides[1 : rows + 1] = left_ref[...].astype(F32)
        sides[rows + 1 : rows + 2] = bottom[0:1]
        sides[24:25] = top[1:2]
        sides[25 : rows + 25] = right_ref[...].astype(F32)
        sides[rows + 25 : rows + 26] = bottom[1:2]

    weight = expand_ref[...]
    block = 3
    for rb in range((rows + 2) // block):
        piece = tokens[rb * block * cols : (rb + 1) * block * cols]
        value = gelu(dot(piece, weight))
        expanded[rb * block : (rb + 1) * block, 1 : steps + 1] = value.reshape(block, steps, SEG, width)
    side_vals[...] = gelu(dot(sides[...].astype(BF16), weight))
    place = lax.broadcasted_iota(jnp.int32, (SEG, width), 0)
    for r in range(rows + 2):
        before = pltpu.roll(expanded[r, steps], 1, 0)
        expanded[r, 0] = jnp.where(place == 0, side_vals[r : r + 1], before)
        after = pltpu.roll(expanded[r, 1], SEG - 1, 0)
        expanded[r, steps + 1] = jnp.where(place == SEG - 1, side_vals[24 + r : 25 + r], after)

    for lt in range(width // 128):
        lanes = slice(lt * 128, (lt + 1) * 128)
        taps = [[dw_ref[3 * i + j : 3 * i + j + 1, lanes].reshape(1, 1, 128) for j in range(3)] for i in range(3)]
        shift = bias_ref[0:1, lanes].reshape(1, 1, 128)

        def one_row(r, _):
            acc = jnp.broadcast_to(shift, (steps, SEG, 128))
            for i in range(3):
                window = expanded[r + i, :, :, lanes]
                for j in range(3):
                    acc = acc + window[j : j + steps] * taps[i][j]
            value = gelu(acc).reshape(cols, 128).astype(BF16)
            mixed[pl.ds(pl.multiple_of(r * cols, cols), cols), lanes] = value
            return 0

        lax.fori_loop(0, rows, one_row, 0, unroll=2)

    branch = dot(mixed[...], project_ref[...])

    @pl.when(step == 0)
    def _():
        total[...] = branch

    @pl.when(step > 0)
    def _():
        total[...] += branch

    @pl.when(step == pl.num_programs(0) - 1)
    def _():
        flag = keep_ref[frame, 0].astype(F32)
        span = order_ref.shape[0]
        groups = span // cols
        stride = rows // groups
        order = order_ref[...]
        for d in range(stride):
            parts = []
            for g in range(groups):
                r = g * stride + d
                residual = tokens[(r + 1) * cols : (r + 2) * cols].astype(F32)
                parts.append((residual + flag * total[r * cols : (r + 1) * cols]).astype(BF16))
            value = parts[0] if groups == 1 else jnp.concatenate(parts, axis=0)
            out_ref[d * span : (d + 1) * span] = dot(order, value).astype(BF16)


def conv_call(frame, keep, x, top, bottom, left, right, seg, order, expand_weight, dw, bias, project_weight):
    rows, cols, channels = x.shape
    hidden = expand_weight.shape[1]
    steps = cols // SEG
    span = order.shape[0]

    def whole(a):
        return pl.BlockSpec(a.shape, lambda e, n=a.ndim: (0,) * n)

    def body(*refs):
        conv_kernel(frame, *refs)

    return pl.pallas_call(
        body,
        grid=(hidden // CHUNK,),
        in_specs=[
            pl.BlockSpec(memory_space=pltpu.SMEM),
            whole(x),
            whole(top),
            whole(bottom),
            whole(left),
            whole(right),
            whole(seg),
            whole(order),
            pl.BlockSpec((channels, CHUNK), lambda e: (0, e)),
            pl.BlockSpec((9, CHUNK), lambda e: (0, e)),
            pl.BlockSpec((1, CHUNK), lambda e: (0, e)),
            pl.BlockSpec((CHUNK, channels), lambda e: (e, 0)),
        ],
        out_specs=pl.BlockSpec((rows * cols, channels), lambda e: (0, 0)),
        out_shape=jax.ShapeDtypeStruct((rows * cols, channels), BF16),
        scratch_shapes=[
            pltpu.VMEM(((rows + 2) * cols, channels), BF16),
            pltpu.VMEM((48, channels), F32),
            pltpu.VMEM((48, CHUNK), F32),
            pltpu.VMEM((rows + 2, steps + 2, SEG, CHUNK), F32),
            pltpu.VMEM((rows * cols, CHUNK), BF16),
            pltpu.VMEM((rows * cols, channels), F32),
        ],
        compiler_params=pltpu.CompilerParams(vmem_limit_bytes=VMEM_LIMIT),
        cost_estimate=pl.CostEstimate(flops=6 * 10**9, bytes_accessed=4 * 10**6, transcendentals=4 * 10**6),
    )(keep, x, top, bottom, left, right, seg, order, expand_weight, dw, bias, project_weight)


def attend_kernel(frame, keep_ref, x_ref, query_ref, key_ref, value_ref, out_w_ref, out_ref, held):
    windows = held.shape[1]
    sources, _, group, channels = held.shape
    count = sources * group
    head_dim = channels // HEADS
    per_tile = 128 // head_dim
    scale = head_dim ** (-0.5) * math.log2(math.e)
    held[...] = x_ref[...].astype(F32).reshape(held.shape)
    flag = keep_ref[frame, 1].astype(F32)

    def one_window(w, _):
        residual = held[:, w].reshape(count, channels)
        normed = normalize(residual).astype(BF16)
        queries = dot_t(query_ref[...], normed).astype(BF16)
        keys_part = dot(normed, key_ref[...]).astype(BF16)
        values_part = dot_t(value_ref[...], normed).astype(BF16)
        outs = []
        for h in range(HEADS):
            tile, inside = h // per_tile, h % per_tile
            query = queries[h * head_dim : (h + 1) * head_dim]
            pieces = []
            if inside > 0:
                pieces.append(jnp.zeros((inside * head_dim, count), BF16))
            pieces.append(query)
            if inside < per_tile - 1:
                pieces.append(jnp.zeros(((per_tile - 1 - inside) * head_dim, count), BF16))
            padded = jnp.concatenate(pieces, axis=0)
            scores = dot(keys_part[:, tile * 128 : (tile + 1) * 128], padded)
            top_score = jnp.max(scores, axis=0, keepdims=True)
            weights = jnp.exp2((scores - top_score) * scale)
            norm = jnp.sum(weights, axis=0, keepdims=True)
            value = values_part[h * head_dim : (h + 1) * head_dim]
            outs.append(dot(value, weights.astype(BF16)) * (1.0 / norm))
        attended = jnp.concatenate(outs, axis=0).T.astype(BF16)
        update = dot(attended, out_w_ref[...])
        held[:, w] = (residual + flag * update).reshape(sources, group, channels)
        return 0

    lax.fori_loop(0, windows, one_window, 0)
    out_ref[...] = held[...].reshape(out_ref.shape).astype(BF16)


def attend_call(frame, keep, x, windows, group, query_w, key_w, value_w, out_weight):
    tokens, channels = x.shape
    held = (tokens // (windows * group), windows, group, channels)

    def body(*refs):
        attend_kernel(frame, *refs)

    return pl.pallas_call(
        body,
        in_specs=[pl.BlockSpec(memory_space=pltpu.SMEM)] + [pl.BlockSpec(memory_space=pltpu.VMEM)] * 5,
        out_specs=pl.BlockSpec(memory_space=pltpu.VMEM),
        out_shape=jax.ShapeDtypeStruct(x.shape, BF16),
        scratch_shapes=[pltpu.VMEM(held, F32)],
        compiler_params=pltpu.CompilerParams(vmem_limit_bytes=VMEM_LIMIT),
        cost_estimate=pl.CostEstimate(flops=6 * 10**9, bytes_accessed=3 * 10**6, transcendentals=4 * 10**6),
    )(keep, x, query_w, key_w, value_w, out_weight)


def mlp_kernel(frame, keep_ref, x_ref, order_ref, in_ref, outw_ref, *rest):
    out_ref = rest[-1]
    _, rows, cols, channels = out_ref.shape
    span = order_ref.shape[0]
    groups = span // cols
    stride = rows // groups
    flag = keep_ref[frame, 2].astype(F32)
    order = order_ref[...]
    for d in range(stride):
        residual = x_ref[d * span : (d + 1) * span].astype(F32)
        normed = normalize(residual).astype(BF16)
        inner = gelu(dot(normed, in_ref[...])).astype(BF16)
        value = (residual + flag * dot(inner, outw_ref[...])).astype(BF16)
        back = dot(order, value).astype(BF16)
        for g in range(groups):
            out_ref[0, g * stride + d] = back[g * cols : (g + 1) * cols]


def mlp_call(frame, keep, x, order, mlp_in, mlp_out, out_shape, previous):
    _, rows, cols, channels = out_shape

    def whole(a):
        return pl.BlockSpec(a.shape, lambda i, n=a.ndim: (0,) * n)

    def body(*refs):
        mlp_kernel(frame, *refs)

    args = [keep, x, order, mlp_in, mlp_out]
    specs = [pl.BlockSpec(memory_space=pltpu.SMEM)] + [whole(a) for a in args[1:]]
    aliases = {}
    if previous is not None:
        aliases = {len(args): 0}
        args.append(previous)
        specs.append(pl.BlockSpec(memory_space=pl.ANY))
    return pl.pallas_call(
        body,
        grid=(1,),
        in_specs=specs,
        out_specs=pl.BlockSpec((1, rows, cols, channels), lambda i: (frame, 0, 0, 0)),
        out_shape=jax.ShapeDtypeStruct(out_shape, BF16),
        input_output_aliases=aliases,
        compiler_params=pltpu.CompilerParams(vmem_limit_bytes=VMEM_LIMIT),
        cost_estimate=pl.CostEstimate(flops=5 * 10**9, bytes_accessed=4 * 10**6, transcendentals=2 * 10**6),
    )(*args)


def body(
    frames,
    keep,
    expand_weight,
    dw_kernel,
    conv_bias,
    project_weight,
    qkv_weight,
    out_weight,
    mlp_in,
    mlp_out,
):
    frame_count, rows, cols, channels = frames.shape
    rows_axis = lax.axis_size("ha")
    cols_axis = lax.axis_size("wa")
    row_stride = rows * rows_axis // GRID
    col_stride = cols * cols_axis // GRID
    assert row_stride == rows_axis and col_stride % cols_axis == 0
    cols_each = col_stride // cols_axis
    row_groups = rows // row_stride
    col_groups = cols // col_stride
    group = row_groups * col_groups
    devices = rows_axis * cols_axis

    right_way = [(i, i + 1) for i in range(cols_axis - 1)]
    left_way = [(j, i) for i, j in right_way]
    left = lax.ppermute(frames[:, :, cols - 1], "wa", right_way)
    right = lax.ppermute(frames[:, :, 0], "wa", left_way)
    down_way = [(i, i + 1) for i in range(rows_axis - 1)]
    up_way = [(j, i) for i, j in down_way]

    def edge(r):
        spare = jnp.zeros((frame_count, 14, channels), BF16)
        return jnp.concatenate([frames[:, r], left[:, r : r + 1], right[:, r : r + 1], spare], axis=1)

    top = lax.ppermute(edge(rows - 1), "ha", down_way)
    bottom = lax.ppermute(edge(0), "ha", up_way)

    to_segments = segment_order(cols, 2)
    to_message = message_order(row_groups, cols, col_stride, cols_each)
    from_segments = np.kron(np.eye(row_groups), segment_order(cols, 1)).T
    seg = jnp.asarray(to_segments, BF16)
    order = jnp.asarray(to_message @ from_segments, BF16)
    order_back = jnp.asarray(to_message.T, BF16)
    dw = dw_kernel.reshape(9, -1)
    bias = conv_bias.reshape(1, -1)
    query_w = qkv_weight[:, :channels].T
    key_w = qkv_weight[:, channels : 2 * channels]
    value_w = qkv_weight[:, 2 * channels :].T

    def exchange(x):
        message = x.reshape(devices, -1, channels)
        return lax.all_to_all(message, ("ha", "wa"), split_axis=0, concat_axis=0, tiled=True).reshape(-1, channels)

    sent = []
    for f in range(frame_count):
        first = conv_call(
            f,
            keep,
            frames[f],
            top[f],
            bottom[f],
            left[f],
            right[f],
            seg,
            order,
            expand_weight,
            dw,
            bias,
            project_weight,
        )
        sent.append(exchange(first))
    back = []
    for f in range(frame_count):
        x = sent[f]
        if group == 8:
            second = attend_call(f, keep, x, cols_each, 8, query_w, key_w, value_w, out_weight)
        else:
            x = x.reshape(devices, cols_each, group, channels).swapaxes(0, 1).reshape(-1, 8, channels)
            x = x.reshape(cols_each, -1, 8, channels).swapaxes(0, 1).reshape(-1, channels)
            second = attend_call(f, keep, x, cols_each, 8, query_w, key_w, value_w, out_weight)
            second = second.reshape(-1, cols_each, 8, channels).swapaxes(0, 1)
            second = second.reshape(cols_each, devices, group, channels).swapaxes(0, 1).reshape(-1, channels)
        back.append(exchange(second))
    result = None
    for f in range(frame_count):
        result = mlp_call(f, keep, back[f], order_back, mlp_in, mlp_out, frames.shape, result)
    return result


def solution(mesh):
    in_specs = (P(None, "ha", "wa", None), P(), P(), P(), P(), P(), P(), P(), P(), P())
    out_specs = P(None, "ha", "wa", None)
    return jax.shard_map(body, mesh=mesh, in_specs=in_specs, out_specs=out_specs, check_vma=False)
```

```python
import math

import jax
import jax.numpy as jnp
import numpy as np
from jax import lax
from jax.experimental import pallas as pl
from jax.experimental.pallas import tpu as pltpu
from jax.sharding import PartitionSpec as P

HEADS = 12
GRID = 16
SEG = 8
CHUNK = 768
F32 = jnp.float32
BF16 = jnp.bfloat16
MIB = 1024 * 1024


def gelu(v):
    cubic = v * (math.sqrt(2 / math.pi) + (math.sqrt(2 / math.pi) * 0.044715) * (v * v))
    half = 0.5 * v
    return half + half * jnp.tanh(cubic)


def half_gelu(h):
    root = math.sqrt(2 / math.pi)
    return h + h * jnp.tanh(h * (2 * root + (8 * root * 0.044715) * (h * h)))


def normalize(values):
    mean_val = jnp.mean(values, axis=-1, keepdims=True)
    centred = values - mean_val
    variance = jnp.mean(centred * centred, axis=-1, keepdims=True)
    return centred * lax.rsqrt(variance + 1e-05)


def dot(a, b):
    return jnp.dot(a, b, preferred_element_type=F32)


def dot_t(a, b):
    return lax.dot_general(a, b, (((1,), (1,)), ((), ())), preferred_element_type=F32)


def segment_order(cols, count):
    steps = cols // SEG
    matrix = np.zeros((count * cols, count * cols), np.float32)
    for row in range(count):
        for t in range(steps):
            for s in range(SEG):
                matrix[row * cols + t * SEG + s, row * cols + s * steps + t] = 1
    return matrix


def message_order(row_groups, cols, col_stride, cols_each):
    col_groups = cols // col_stride
    dests = col_stride // cols_each
    matrix = np.zeros((row_groups * cols, row_groups * cols), np.float32)
    place = 0
    for w in range(dests):
        for b in range(cols_each):
            for g in range(row_groups):
                for h in range(col_groups):
                    matrix[place, g * cols + h * col_stride + w * cols_each + b] = 1
                    place += 1
    return matrix


def conv_kernel(
    frame,
    keep_ref,
    dw_any,
    bias_any,
    seg_any,
    order_any,
    x_any,
    top_any,
    bottom_any,
    left_any,
    right_any,
    expand_any,
    project_any,
    out_ref,
    x_ref,
    top_ref,
    bottom_ref,
    left_ref,
    right_ref,
    expand_ref,
    project_ref,
    dw_ref,
    bias_ref,
    seg_ref,
    order_ref,
    sems,
    tokens,
    sides,
    side_vals,
    taps,
    expanded,
    mixed,
    total,
):
    rows, cols, channels = x_ref.shape
    steps = cols // SEG
    hidden = expand_ref.shape[1]
    chunks = hidden // CHUNK
    pairs = [
        (x_any.at[frame], x_ref),
        (expand_any, expand_ref),
        (top_any.at[frame], top_ref),
        (bottom_any.at[frame], bottom_ref),
        (left_any.at[frame], left_ref),
        (right_any.at[frame], right_ref),
        (project_any, project_ref),
        (seg_any, seg_ref),
        (dw_any, dw_ref),
        (bias_any, bias_ref),
        (order_any, order_ref),
    ]
    copies = [pltpu.make_async_copy(src, dst, sems.at[i]) for i, (src, dst) in enumerate(pairs)]
    for copy in copies:
        copy.start()
    sides[...] = jnp.zeros_like(sides)
    copies[7].wait()
    seg_pair = seg_ref[...]
    seg_one = seg_pair[:cols, :cols]
    copies[0].wait()
    pair = 2 * cols
    for r in range(rows // 2):
        both = x_ref[2 * r : 2 * r + 2].reshape(pair, channels)
        tokens[cols + r * pair : cols + (r + 1) * pair] = dot(seg_pair, both).astype(BF16)
    for copy in copies[2:6]:
        copy.wait()
    tokens[0:cols] = dot(seg_one, top_ref[0:cols]).astype(BF16)
    tokens[(rows + 1) * cols : (rows + 2) * cols] = dot(seg_one, bottom_ref[0:cols]).astype(BF16)
    top = 0.5 * top_ref[cols : cols + 16].astype(F32)
    bottom = 0.5 * bottom_ref[cols : cols + 16].astype(F32)
    sides[0:1] = top[0:1]
    sides[1 : rows + 1] = 0.5 * left_ref[...].astype(F32)
    sides[rows + 1 : rows + 2] = bottom[0:1]
    sides[24:25] = top[1:2]
    sides[25 : rows + 25] = 0.5 * right_ref[...].astype(F32)
    sides[rows + 25 : rows + 26] = bottom[1:2]
    copies[1].wait()
    place = lax.broadcasted_iota(jnp.int32, (SEG, CHUNK), 0)

    def expand_sides(c):
        lanes = slice(c * CHUNK, (c + 1) * CHUNK)
        side_vals[:, lanes] = half_gelu(dot(sides[...].astype(BF16), expand_ref[:, lanes]))

    def expand_rows(c, start, stop):
        lanes = slice(c * CHUNK, (c + 1) * CHUNK)
        value = half_gelu(dot(tokens[start * cols : stop * cols], expand_ref[:, lanes]))
        value = value.reshape(stop - start, steps, SEG, CHUNK)
        expanded[start:stop, 1 : steps + 1, :, lanes] = value
        for r in range(start, stop):
            before = pltpu.roll(value[r - start, steps - 1], 1, 0)
            expanded[r, 0, :, lanes] = jnp.where(place == 0, side_vals[r : r + 1, lanes], before)
            after = pltpu.roll(value[r - start, 0], SEG - 1, 0)
            expanded[r, steps + 1, :, lanes] = jnp.where(place == SEG - 1, side_vals[24 + r : 25 + r, lanes], after)

    def conv_row(c, r):
        for lt in range(CHUNK // 128):
            lanes = slice(c * CHUNK + lt * 128, c * CHUNK + (lt + 1) * 128)
            acc = jnp.broadcast_to(taps[9:10, lanes].reshape(1, 1, 128), (steps, SEG, 128))
            for i in range(3):
                window = expanded[r + i, :, :, lanes]
                for j in range(3):
                    acc = acc + window[j : j + steps] * taps[3 * i + j : 3 * i + j + 1, lanes].reshape(1, 1, 128)
            mixed[r * cols : (r + 1) * cols, lanes] = half_gelu(acc).reshape(cols, 128).astype(BF16)

    def project_rows(c, start, stop):
        lanes = slice(c * CHUNK, (c + 1) * CHUNK)
        span = slice(start * cols, stop * cols)
        branch = dot(mixed[span, lanes], project_ref[lanes])
        total[span] = branch if c == 0 else total[span] + branch

    block = 6
    part = rows // 2
    expand_sides(0)
    for start in range(0, rows + 2, block):
        expand_rows(0, start, start + block)
    for copy in copies[8:11]:
        copy.wait()
    for i in range(3):
        taps[3 * i : 3 * i + 3] = 0.5 * dw_ref[i]
    taps[9:10] = 0.5 * bias_ref[...].reshape(1, hidden)
    copies[6].wait()
    for c in range(chunks):
        if c + 1 < chunks:
            expand_sides(c + 1)
        for r in range(rows):
            conv_row(c, r)
            if c + 1 < chunks and r % block == block - 1:
                expand_rows(c + 1, r + 1 - block, r + 1)
            if r % part == part - 1 and r >= part:
                project_rows(c, r + 1 - 2 * part, r + 1 - part)
        if c + 1 < chunks:
            expand_rows(c + 1, rows // block * block, rows + 2)
        project_rows(c, rows - part, rows)

    flag = keep_ref[frame, 0].astype(F32)
    span = order_ref.shape[0]
    groups = span // cols
    stride = rows // groups
    order = order_ref[...]
    for d in range(stride):
        parts = []
        for g in range(groups):
            r = g * stride + d
            residual = 2.0 * tokens[(r + 1) * cols : (r + 2) * cols].astype(F32)
            parts.append((residual + flag * total[r * cols : (r + 1) * cols]).astype(BF16))
        value = parts[0] if groups == 1 else jnp.concatenate(parts, axis=0)
        out_ref[d * span : (d + 1) * span] = dot(order, value).astype(BF16)


def conv_call(frame, keep, x, top, bottom, left, right, seg, order, expand_weight, dw, bias, project_weight):
    _, rows, cols, channels = x.shape
    hidden = expand_weight.shape[1]
    steps = cols // SEG

    def body(*refs):
        conv_kernel(frame, *refs)

    own = [pltpu.VMEM(a.shape[1:], BF16) for a in (x, top, bottom, left, right)]
    return pl.pallas_call(
        body,
        in_specs=[pl.BlockSpec(memory_space=pltpu.SMEM)]
        + [pl.BlockSpec(memory_space=pl.ANY)] * 11,
        out_specs=pl.BlockSpec(memory_space=pltpu.VMEM),
        out_shape=jax.ShapeDtypeStruct((rows * cols, channels), BF16),
        scratch_shapes=own
        + [
            pltpu.VMEM(expand_weight.shape, BF16),
            pltpu.VMEM(project_weight.shape, BF16),
            pltpu.VMEM(dw.shape, F32),
            pltpu.VMEM(bias.shape, F32),
            pltpu.VMEM(seg.shape, BF16),
            pltpu.VMEM(order.shape, BF16),
            pltpu.SemaphoreType.DMA((11,)),
            pltpu.VMEM(((rows + 2) * cols, channels), BF16),
            pltpu.VMEM((48, channels), F32),
            pltpu.VMEM((48, hidden), F32),
            pltpu.VMEM((16, hidden), F32),
            pltpu.VMEM((rows + 2, steps + 2, SEG, hidden), F32),
            pltpu.VMEM((rows * cols, hidden), BF16),
            pltpu.VMEM((rows * cols, channels), F32),
        ],
        compiler_params=pltpu.CompilerParams(vmem_limit_bytes=60 * MIB),
        cost_estimate=pl.CostEstimate(flops=6 * 10**9, bytes_accessed=4 * 10**6, transcendentals=4 * 10**6),
    )(keep, dw, bias, seg, order, x, top, bottom, left, right, expand_weight, project_weight)


def window_kernel(frame, keep_ref, x_ref, qkv_ref, out_w_ref, in_ref, down_ref, out_ref, held):
    windows = held.shape[1]
    sources, _, group, channels = held.shape
    count = sources * group
    head_dim = channels // HEADS
    per_tile = 128 // head_dim
    scale = head_dim ** (-0.5) * math.log2(math.e)
    held[...] = x_ref[...].astype(F32).reshape(held.shape)
    attend_flag = keep_ref[frame, 1].astype(F32)
    mlp_flag = keep_ref[frame, 2].astype(F32)
    head_of_lane = lax.broadcasted_iota(jnp.int32, (1, 128), 1) // head_dim
    ones = jnp.ones((count, 128), BF16)
    none = jnp.zeros((), BF16)

    def attend(residual):
        qkv = dot(normalize(residual).astype(BF16), qkv_ref[...]).astype(BF16)
        tiles = []
        for t in range(channels // 128):
            queries = qkv[:, t * 128 : (t + 1) * 128]
            keys_part = qkv[:, channels + t * 128 : channels + (t + 1) * 128]
            values_part = qkv[:, 2 * channels + t * 128 : 2 * channels + (t + 1) * 128]
            values_part = jnp.concatenate([values_part, ones], axis=1)
            tile = None
            for i in range(per_tile):
                scores = dot_t(jnp.where(head_of_lane == i, queries, none), keys_part)
                top_score = jnp.max(scores, axis=1, keepdims=True)
                weights = jnp.exp2((scores - top_score) * scale).astype(BF16)
                both = dot(weights, values_part)
                share = both[:, :128] * (1.0 / both[:, 128:])
                tile = share if tile is None else jnp.where(head_of_lane == i, share, tile)
            tiles.append(tile.astype(BF16))
        update = dot(jnp.concatenate(tiles, axis=1), out_w_ref[...])
        return (residual + attend_flag * update).astype(BF16).astype(F32)

    def mlp(residual):
        inner = gelu(dot(normalize(residual).astype(BF16), in_ref[...])).astype(BF16)
        return residual + mlp_flag * dot(inner, down_ref[...])

    second = None
    for w in range(windows + 1):
        if second is not None:
            held[:, w - 1] = mlp(second).reshape(sources, group, channels)
        if w < windows:
            second = attend(held[:, w].reshape(count, channels))
    out_ref[...] = held[...].reshape(out_ref.shape).astype(BF16)


def window_call(frame, keep, x, windows, group, qkv_weight, out_weight, mlp_in, mlp_out):
    tokens, channels = x.shape
    held = (tokens // (windows * group), windows, group, channels)

    def body(*refs):
        window_kernel(frame, *refs)

    return pl.pallas_call(
        body,
        in_specs=[pl.BlockSpec(memory_space=pltpu.SMEM)] + [pl.BlockSpec(memory_space=pltpu.VMEM)] * 5,
        out_specs=pl.BlockSpec(memory_space=pltpu.VMEM),
        out_shape=jax.ShapeDtypeStruct(x.shape, BF16),
        scratch_shapes=[pltpu.VMEM(held, F32)],
        compiler_params=pltpu.CompilerParams(vmem_limit_bytes=40 * MIB),
        cost_estimate=pl.CostEstimate(flops=9 * 10**9, bytes_accessed=4 * 10**6, transcendentals=6 * 10**6),
    )(keep, x, qkv_weight, out_weight, mlp_in, mlp_out)


def restore_kernel(x_ref, order_ref, *rest):
    out_ref = rest[-1]
    _, rows, cols, channels = out_ref.shape
    span = order_ref.shape[0]
    groups = span // cols
    stride = rows // groups
    order = order_ref[...]
    for d in range(stride):
        back = dot(order, x_ref[d * span : (d + 1) * span]).astype(BF16)
        for g in range(groups):
            out_ref[0, g * stride + d] = back[g * cols : (g + 1) * cols]


def restore_call(frame, x, order, out_shape, previous):
    _, rows, cols, channels = out_shape

    def whole(a):
        return pl.BlockSpec(a.shape, lambda i, n=a.ndim: (0,) * n)

    args = [x, order]
    specs = [whole(a) for a in args]
    aliases = {}
    if previous is not None:
        aliases = {len(args): 0}
        args.append(previous)
        specs.append(pl.BlockSpec(memory_space=pl.ANY))
    return pl.pallas_call(
        restore_kernel,
        grid=(1,),
        in_specs=specs,
        out_specs=pl.BlockSpec((1, rows, cols, channels), lambda i: (frame, 0, 0, 0)),
        out_shape=jax.ShapeDtypeStruct(out_shape, BF16),
        input_output_aliases=aliases,
        compiler_params=pltpu.CompilerParams(vmem_limit_bytes=16 * MIB),
        cost_estimate=pl.CostEstimate(flops=10**8, bytes_accessed=2 * 10**6, transcendentals=0),
    )(*args)


def neighbours(first, last, axis):
    size = lax.axis_size(axis)
    even = lax.axis_index(axis) % 2 == 0
    inner = [(i, i ^ 1) for i in range(size)]
    outer = [(i, i + 1) for i in range(1, size - 1, 2)]
    outer = outer + [(j, i) for i, j in outer]
    across = lax.ppermute(jnp.where(even, first, last), axis, outer)
    within = lax.ppermute(jnp.where(even, last, first), axis, inner)
    return jnp.where(even, across, within), jnp.where(even, within, across)


def body(
    frames,
    keep,
    expand_weight,
    dw_kernel,
    conv_bias,
    project_weight,
    qkv_weight,
    out_weight,
    mlp_in,
    mlp_out,
):
    frame_count, rows, cols, channels = frames.shape
    rows_axis = lax.axis_size("ha")
    cols_axis = lax.axis_size("wa")
    row_stride = rows * rows_axis // GRID
    col_stride = cols * cols_axis // GRID
    assert row_stride == rows_axis and col_stride % cols_axis == 0
    cols_each = col_stride // cols_axis
    row_groups = rows // row_stride
    col_groups = cols // col_stride
    group = row_groups * col_groups
    devices = rows_axis * cols_axis

    left, right = neighbours(frames[:, :, 0], frames[:, :, cols - 1], "wa")

    def edge(r):
        spare = jnp.zeros((frame_count, 14, channels), BF16)
        return jnp.concatenate([frames[:, r], left[:, r : r + 1], right[:, r : r + 1], spare], axis=1)

    top, bottom = neighbours(edge(0), edge(rows - 1), "ha")

    to_segments = segment_order(cols, 2)
    to_message = message_order(row_groups, cols, col_stride, cols_each)
    from_segments = np.kron(np.eye(row_groups), segment_order(cols, 1)).T
    seg = jnp.asarray(0.5 * to_segments, BF16)
    order = jnp.asarray(to_message @ from_segments, BF16)
    order_back = jnp.asarray(to_message.T, BF16)
    def exchange(x):
        message = x.reshape(devices, -1, channels)
        return lax.all_to_all(message, ("ha", "wa"), split_axis=0, concat_axis=0, tiled=True).reshape(-1, channels)

    sent = []
    for f in range(frame_count):
        first = conv_call(
            f,
            keep,
            frames,
            top,
            bottom,
            left,
            right,
            seg,
            order,
            expand_weight,
            dw_kernel,
            conv_bias,
            project_weight,
        )
        sent.append(exchange(first))
    back = []
    for f in range(frame_count):
        x = sent[f]
        if group != 8:
            x = x.reshape(devices, cols_each, group, channels).swapaxes(0, 1).reshape(cols_each, -1, 8, channels)
            x = x.swapaxes(0, 1).reshape(-1, channels)
        x = window_call(f, keep, x, cols_each, 8, qkv_weight, out_weight, mlp_in, mlp_out)
        if group != 8:
            x = x.reshape(-1, cols_each, 8, channels).swapaxes(0, 1).reshape(cols_each, devices, group, channels)
            x = x.swapaxes(0, 1).reshape(-1, channels)
        back.append(exchange(x))
    result = None
    for f in range(frame_count):
        result = restore_call(f, back[f], order_back, frames.shape, result)
    return result


def solution(mesh):
    in_specs = (P(None, "ha", "wa", None), P(), P(), P(), P(), P(), P(), P(), P(), P())
    out_specs = P(None, "ha", "wa", None)
    return jax.shard_map(body, mesh=mesh, in_specs=in_specs, out_specs=out_specs, check_vma=False)
```

```python
import math

import jax
import jax.numpy as jnp
import numpy as np
from jax import lax
from jax.experimental import pallas as pl
from jax.experimental.pallas import tpu as pltpu
from jax.sharding import PartitionSpec as P

HEADS = 12
GRID = 16
SEG = 8
CHUNK = 768
F32 = jnp.float32
BF16 = jnp.bfloat16
MIB = 1024 * 1024


def gelu(v):
    cubic = v * (math.sqrt(2 / math.pi) + (math.sqrt(2 / math.pi) * 0.044715) * (v * v))
    half = 0.5 * v
    return half + half * jnp.tanh(cubic)


def half_gelu(h):
    root = math.sqrt(2 / math.pi)
    return h + h * jnp.tanh(h * (2 * root + (8 * root * 0.044715) * (h * h)))


def normalize(values):
    mean_val = jnp.mean(values, axis=-1, keepdims=True)
    centred = values - mean_val
    variance = jnp.mean(centred * centred, axis=-1, keepdims=True)
    return centred * lax.rsqrt(variance + 1e-05)


def dot(a, b):
    return jnp.dot(a, b, preferred_element_type=F32)


def dot_t(a, b):
    return lax.dot_general(a, b, (((1,), (1,)), ((), ())), preferred_element_type=F32)


def segment_order(cols, count):
    steps = cols // SEG
    matrix = np.zeros((count * cols, count * cols), np.float32)
    for row in range(count):
        for t in range(steps):
            for s in range(SEG):
                matrix[row * cols + t * SEG + s, row * cols + s * steps + t] = 1
    return matrix


def message_order(row_groups, cols, col_stride, cols_each):
    col_groups = cols // col_stride
    dests = col_stride // cols_each
    matrix = np.zeros((row_groups * cols, row_groups * cols), np.float32)
    place = 0
    for w in range(dests):
        for b in range(cols_each):
            for g in range(row_groups):
                for h in range(col_groups):
                    matrix[place, g * cols + h * col_stride + w * cols_each + b] = 1
                    place += 1
    return matrix


def expand_kernel(frame, seg_any, x_any, expand_any, expanded, tokens, x_ref, expand_ref, seg_ref, sems):
    rows, steps, _, hidden = expanded.shape
    cols = steps * SEG
    channels = x_ref.shape[-1]
    pairs = [(seg_any, seg_ref), (x_any.at[frame], x_ref), (expand_any, expand_ref)]
    copies = [pltpu.make_async_copy(src, dst, sems.at[i]) for i, (src, dst) in enumerate(pairs)]
    for copy in copies:
        copy.start()
    copies[0].wait()
    copies[1].wait()
    pair = 2 * cols
    for r in range(rows // 2):
        both = x_ref[2 * r : 2 * r + 2].reshape(pair, channels)
        tokens[r * pair : (r + 1) * pair] = dot(seg_ref[...], both).astype(BF16)
    copies[2].wait()
    block = 4
    for c in range(hidden // CHUNK):
        lanes = slice(c * CHUNK, (c + 1) * CHUNK)
        for r in range(0, rows, block):
            value = half_gelu(dot(tokens[r * cols : (r + block) * cols], expand_ref[:, lanes]))
            expanded[r : r + block, :, :, lanes] = value.reshape(block, steps, SEG, CHUNK)


def expand_call(frame, seg, x, expand_weight):
    _, rows, cols, channels = x.shape
    hidden = expand_weight.shape[1]

    def body(*refs):
        expand_kernel(frame, *refs)

    return pl.pallas_call(
        body,
        in_specs=[pl.BlockSpec(memory_space=pl.ANY)] * 3,
        out_specs=[pl.BlockSpec(memory_space=pltpu.VMEM)] * 2,
        out_shape=[
            jax.ShapeDtypeStruct((rows, cols // SEG, SEG, hidden), F32),
            jax.ShapeDtypeStruct((rows * cols, channels), BF16),
        ],
        scratch_shapes=[
            pltpu.VMEM(x.shape[1:], BF16),
            pltpu.VMEM(expand_weight.shape, BF16),
            pltpu.VMEM(seg.shape, BF16),
            pltpu.SemaphoreType.DMA((3,)),
        ],
        compiler_params=pltpu.CompilerParams(vmem_limit_bytes=24 * MIB),
        cost_estimate=pl.CostEstimate(flops=3 * 10**9, bytes_accessed=4 * 10**6, transcendentals=2 * 10**6),
    )(seg, x, expand_weight)


def conv_kernel(
    frame,
    keep_ref,
    even_ref,
    own_ref,
    tokens,
    dw_any,
    bias_any,
    seg_any,
    order_any,
    outer_rows_any,
    inner_rows_any,
    outer_cols_any,
    inner_cols_any,
    expand_any,
    project_any,
    out_ref,
    dw_ref,
    bias_ref,
    seg_ref,
    order_ref,
    outer_rows,
    inner_rows,
    outer_cols,
    inner_cols,
    expand_ref,
    project_ref,
    sems,
    sides,
    side_vals,
    taps,
    edge_cols,
    edge_rows,
    mixed,
    total,
):
    rows, steps, _, hidden = own_ref.shape
    cols = steps * SEG
    pairs = [
        (outer_rows_any.at[frame], outer_rows),
        (inner_rows_any.at[frame], inner_rows),
        (outer_cols_any.at[frame], outer_cols),
        (inner_cols_any.at[frame], inner_cols),
        (seg_any, seg_ref),
        (expand_any, expand_ref),
        (dw_any, dw_ref),
        (bias_any, bias_ref),
        (project_any, project_ref),
        (order_any, order_ref),
    ]
    copies = [pltpu.make_async_copy(src, dst, sems.at[i]) for i, (src, dst) in enumerate(pairs)]
    for copy in copies:
        copy.start()
    sides[...] = jnp.zeros_like(sides)
    for copy in copies[0:5]:
        copy.wait()
    even_row, even_col = even_ref[0] == 1, even_ref[1] == 1
    outer, inner = outer_rows[...], inner_rows[...]
    top, bottom = jnp.where(even_row, outer, inner), jnp.where(even_row, inner, outer)
    outer, inner = outer_cols[...], inner_cols[...]
    left, right = jnp.where(even_col, outer, inner), jnp.where(even_col, inner, outer)
    seg_one = seg_ref[:cols, :cols]
    top_tokens = dot(seg_one, top[0:cols]).astype(BF16)
    bottom_tokens = dot(seg_one, bottom[0:cols]).astype(BF16)
    top = 0.5 * top[cols : cols + 16].astype(F32)
    bottom = 0.5 * bottom[cols : cols + 16].astype(F32)
    sides[0:1] = top[0:1]
    sides[1 : rows + 1] = 0.5 * left.astype(F32)
    sides[rows + 1 : rows + 2] = bottom[0:1]
    sides[24:25] = top[1:2]
    sides[25 : rows + 25] = 0.5 * right.astype(F32)
    sides[rows + 25 : rows + 26] = bottom[1:2]
    halo = jnp.concatenate([top_tokens, bottom_tokens, sides[...].astype(BF16)], axis=0)
    place = lax.broadcasted_iota(jnp.int32, (SEG, CHUNK), 0)
    for copy in copies[5:8]:
        copy.wait()
    for i in range(3):
        taps[3 * i : 3 * i + 3] = 0.5 * dw_ref[i]
    taps[9:10] = 0.5 * bias_ref[...].reshape(1, hidden)

    def expand_halo(c):
        lanes = slice(c * CHUNK, (c + 1) * CHUNK)
        value = half_gelu(dot(halo, expand_ref[:, lanes]))
        edge_rows[:, :, :, lanes] = value[: 2 * cols].reshape(2, steps, SEG, CHUNK)
        side_vals[:, lanes] = value[2 * cols :]

    def plain(r, t, lanes):
        if r == 0:
            return edge_rows[0, t, :, lanes]
        if r == rows + 1:
            return edge_rows[1, t, :, lanes]
        return own_ref[r - 1, t, :, lanes]

    def fill_edges(c, r):
        lanes = slice(c * CHUNK, (c + 1) * CHUNK)
        before = pltpu.roll(plain(r, steps - 1, lanes), 1, 0)
        edge_cols[r, 0, :, lanes] = jnp.where(place == 0, side_vals[r : r + 1, lanes], before)
        after = pltpu.roll(plain(r, 0, lanes), SEG - 1, 0)
        edge_cols[r, 1, :, lanes] = jnp.where(place == SEG - 1, side_vals[24 + r : 25 + r, lanes], after)

    def conv_row(c, r):
        for lt in range(CHUNK // 128):
            lanes = slice(c * CHUNK + lt * 128, c * CHUNK + (lt + 1) * 128)
            acc = jnp.broadcast_to(taps[9:10, lanes].reshape(1, 1, 128), (steps, SEG, 128))
            for i in range(3):
                if r + i == 0:
                    middle = edge_rows[0, :, :, lanes]
                elif r + i == rows + 1:
                    middle = edge_rows[1, :, :, lanes]
                else:
                    middle = own_ref[r + i - 1, :, :, lanes]
                window = jnp.concatenate(
                    [edge_cols[r + i, 0:1, :, lanes], middle, edge_cols[r + i, 1:2, :, lanes]], axis=0
                )
                for j in range(3):
                    acc = acc + window[j : j + steps] * taps[3 * i + j : 3 * i + j + 1, lanes].reshape(1, 1, 128)
            mixed[r * cols : (r + 1) * cols, lanes] = half_gelu(acc).reshape(cols, 128).astype(BF16)

    def project_rows(c, start, stop):
        lanes = slice(c * CHUNK, (c + 1) * CHUNK)
        span = slice(start * cols, stop * cols)
        branch = dot(mixed[span, lanes], project_ref[lanes])
        total[span] = branch if c == 0 else total[span] + branch

    part = rows // 2
    for c in range(hidden // CHUNK):
        expand_halo(c)
        if c == 0:
            copies[8].wait()
            copies[9].wait()
        fill_edges(c, 0)
        fill_edges(c, 1)
        for r in range(rows):
            fill_edges(c, r + 2)
            conv_row(c, r)
            if r % part == part - 1 and r >= part:
                project_rows(c, r + 1 - 2 * part, r + 1 - part)
        project_rows(c, rows - part, rows)

    flag = keep_ref[frame, 0].astype(F32)
    span = order_ref.shape[0]
    groups = span // cols
    stride = rows // groups
    order = order_ref[...]
    for d in range(stride):
        parts = []
        for g in range(groups):
            r = g * stride + d
            residual = 2.0 * tokens[r * cols : (r + 1) * cols].astype(F32)
            parts.append((residual + flag * total[r * cols : (r + 1) * cols]).astype(BF16))
        value = parts[0] if groups == 1 else jnp.concatenate(parts, axis=0)
        out_ref[d * span : (d + 1) * span] = dot(order, value).astype(BF16)


def conv_call(frame, keep, even, own, tokens, dw, bias, seg, order, halo, expand_weight, project_weight):
    rows, steps, _, hidden = own.shape
    cols = steps * SEG
    channels = tokens.shape[1]
    large = [dw, bias, seg, order, *halo, expand_weight, project_weight]

    def body(*refs):
        conv_kernel(frame, *refs)

    def buffer(a, k):
        return pltpu.VMEM(a.shape[1:] if 4 <= k < 8 else a.shape, a.dtype)

    return pl.pallas_call(
        body,
        in_specs=[pl.BlockSpec(memory_space=pltpu.SMEM)] * 2
        + [pl.BlockSpec(memory_space=pltpu.VMEM)] * 2
        + [pl.BlockSpec(memory_space=pl.ANY)] * len(large),
        out_specs=pl.BlockSpec(memory_space=pltpu.VMEM),
        out_shape=jax.ShapeDtypeStruct((rows * cols, channels), BF16),
        scratch_shapes=[buffer(a, k) for k, a in enumerate(large)]
        + [
            pltpu.SemaphoreType.DMA((len(large),)),
            pltpu.VMEM((48, channels), F32),
            pltpu.VMEM((48, hidden), F32),
            pltpu.VMEM((16, hidden), F32),
            pltpu.VMEM((rows + 2, 2, SEG, hidden), F32),
            pltpu.VMEM((2, steps, SEG, hidden), F32),
            pltpu.VMEM((rows * cols, hidden), BF16),
            pltpu.VMEM((rows * cols, channels), F32),
        ],
        compiler_params=pltpu.CompilerParams(vmem_limit_bytes=32 * MIB),
        cost_estimate=pl.CostEstimate(flops=4 * 10**9, bytes_accessed=4 * 10**6, transcendentals=2 * 10**6),
    )(keep, even, own, tokens, *large)


def window_kernel(frame, keep_ref, x_ref, qkv_ref, out_w_ref, in_ref, down_ref, out_ref, held):
    windows = held.shape[1]
    sources, _, group, channels = held.shape
    count = sources * group
    head_dim = channels // HEADS
    per_tile = 128 // head_dim
    scale = head_dim ** (-0.5) * math.log2(math.e)
    held[...] = x_ref[...].astype(F32).reshape(held.shape)
    attend_flag = keep_ref[frame, 1].astype(F32)
    mlp_flag = keep_ref[frame, 2].astype(F32)
    head_of_lane = lax.broadcasted_iota(jnp.int32, (1, 128), 1) // head_dim
    ones = jnp.ones((count, 128), BF16)
    none = jnp.zeros((), BF16)

    def attend(residual):
        qkv = dot(normalize(residual).astype(BF16), qkv_ref[...]).astype(BF16)
        tiles = []
        for t in range(channels // 128):
            queries = qkv[:, t * 128 : (t + 1) * 128]
            keys_part = qkv[:, channels + t * 128 : channels + (t + 1) * 128]
            values_part = qkv[:, 2 * channels + t * 128 : 2 * channels + (t + 1) * 128]
            values_part = jnp.concatenate([values_part, ones], axis=1)
            tile = None
            for i in range(per_tile):
                scores = dot_t(jnp.where(head_of_lane == i, queries, none), keys_part)
                top_score = jnp.max(scores, axis=1, keepdims=True)
                weights = jnp.exp2((scores - top_score) * scale).astype(BF16)
                both = dot(weights, values_part)
                share = both[:, :128] * (1.0 / both[:, 128:])
                tile = share if tile is None else jnp.where(head_of_lane == i, share, tile)
            tiles.append(tile.astype(BF16))
        update = dot(jnp.concatenate(tiles, axis=1), out_w_ref[...])
        return (residual + attend_flag * update).astype(BF16).astype(F32)

    def mlp(residual):
        inner = gelu(dot(normalize(residual).astype(BF16), in_ref[...])).astype(BF16)
        return residual + mlp_flag * dot(inner, down_ref[...])

    def one_window(w, _):
        second = attend(held[:, w].reshape(count, channels))
        held[:, w] = mlp(second).reshape(sources, group, channels)
        return 0

    lax.fori_loop(0, windows, one_window, 0)
    out_ref[...] = held[...].reshape(out_ref.shape).astype(BF16)


def window_call(frame, keep, x, windows, group, qkv_weight, out_weight, mlp_in, mlp_out):
    tokens, channels = x.shape
    held = (tokens // (windows * group), windows, group, channels)

    def body(*refs):
        window_kernel(frame, *refs)

    return pl.pallas_call(
        body,
        in_specs=[pl.BlockSpec(memory_space=pltpu.SMEM)] + [pl.BlockSpec(memory_space=pltpu.VMEM)] * 5,
        out_specs=pl.BlockSpec(memory_space=pltpu.VMEM),
        out_shape=jax.ShapeDtypeStruct(x.shape, BF16),
        scratch_shapes=[pltpu.VMEM(held, F32)],
        compiler_params=pltpu.CompilerParams(vmem_limit_bytes=40 * MIB),
        cost_estimate=pl.CostEstimate(flops=9 * 10**9, bytes_accessed=4 * 10**6, transcendentals=6 * 10**6),
    )(keep, x, qkv_weight, out_weight, mlp_in, mlp_out)


def restore_kernel(x_ref, order_ref, *rest):
    out_ref = rest[-1]
    _, rows, cols, channels = out_ref.shape
    span = order_ref.shape[0]
    groups = span // cols
    stride = rows // groups
    order = order_ref[...]
    for d in range(stride):
        back = dot(order, x_ref[d * span : (d + 1) * span]).astype(BF16)
        for g in range(groups):
            out_ref[0, g * stride + d] = back[g * cols : (g + 1) * cols]


def restore_call(frame, x, order, out_shape, previous):
    _, rows, cols, channels = out_shape

    def whole(a):
        return pl.BlockSpec(a.shape, lambda i, n=a.ndim: (0,) * n)

    args = [x, order]
    specs = [whole(a) for a in args]
    aliases = {}
    if previous is not None:
        aliases = {len(args): 0}
        args.append(previous)
        specs.append(pl.BlockSpec(memory_space=pl.ANY))
    return pl.pallas_call(
        restore_kernel,
        grid=(1,),
        in_specs=specs,
        out_specs=pl.BlockSpec((1, rows, cols, channels), lambda i: (frame, 0, 0, 0)),
        out_shape=jax.ShapeDtypeStruct(out_shape, BF16),
        input_output_aliases=aliases,
        compiler_params=pltpu.CompilerParams(vmem_limit_bytes=16 * MIB),
        cost_estimate=pl.CostEstimate(flops=10**8, bytes_accessed=2 * 10**6, transcendentals=0),
    )(*args)


def neighbours(first, last, axis):
    size = lax.axis_size(axis)
    even = lax.axis_index(axis) % 2 == 0
    inner = [(i, i ^ 1) for i in range(size)]
    outer = [(i, i + 1) for i in range(1, size - 1, 2)]
    outer = outer + [(j, i) for i, j in outer]
    across = lax.ppermute(jnp.where(even, first, last), axis, outer)
    within = lax.ppermute(jnp.where(even, last, first), axis, inner)
    return even, across, within


def body(
    frames,
    keep,
    expand_weight,
    dw_kernel,
    conv_bias,
    project_weight,
    qkv_weight,
    out_weight,
    mlp_in,
    mlp_out,
):
    frame_count, rows, cols, channels = frames.shape
    rows_axis = lax.axis_size("ha")
    cols_axis = lax.axis_size("wa")
    row_stride = rows * rows_axis // GRID
    col_stride = cols * cols_axis // GRID
    assert row_stride == rows_axis and col_stride % cols_axis == 0
    cols_each = col_stride // cols_axis
    row_groups = rows // row_stride
    col_groups = cols // col_stride
    group = row_groups * col_groups
    devices = rows_axis * cols_axis

    even_col, outer_cols, inner_cols = neighbours(frames[:, :, 0], frames[:, :, cols - 1], "wa")
    left = jnp.where(even_col, outer_cols, inner_cols)
    right = jnp.where(even_col, inner_cols, outer_cols)

    def edge(r):
        spare = jnp.zeros((frame_count, 14, channels), BF16)
        return jnp.concatenate([frames[:, r], left[:, r : r + 1], right[:, r : r + 1], spare], axis=1)

    even_row, outer_rows, inner_rows = neighbours(edge(0), edge(rows - 1), "ha")
    halo = (outer_rows, inner_rows, outer_cols, inner_cols)
    even = jnp.stack([even_row, even_col]).astype(jnp.int32)

    to_segments = segment_order(cols, 2)
    to_message = message_order(row_groups, cols, col_stride, cols_each)
    from_segments = np.kron(np.eye(row_groups), segment_order(cols, 1)).T
    seg = jnp.asarray(0.5 * to_segments, BF16)
    order = jnp.asarray(to_message @ from_segments, BF16)
    order_back = jnp.asarray(to_message.T, BF16)
    def exchange(x):
        message = x.reshape(devices, -1, channels)
        return lax.all_to_all(message, ("ha", "wa"), split_axis=0, concat_axis=0, tiled=True).reshape(-1, channels)

    sent = []
    for f in range(frame_count):
        own, tokens = expand_call(f, seg, frames, expand_weight)
        first = conv_call(
            f, keep, even, own, tokens, dw_kernel, conv_bias, seg, order, halo, expand_weight, project_weight
        )
        sent.append(exchange(first))
    back = []
    for f in range(frame_count):
        x = sent[f]
        if group != 8:
            x = x.reshape(devices, cols_each, group, channels).swapaxes(0, 1).reshape(cols_each, -1, 8, channels)
            x = x.swapaxes(0, 1).reshape(-1, channels)
        x = window_call(f, keep, x, cols_each, 8, qkv_weight, out_weight, mlp_in, mlp_out)
        if group != 8:
            x = x.reshape(-1, cols_each, 8, channels).swapaxes(0, 1).reshape(cols_each, devices, group, channels)
            x = x.swapaxes(0, 1).reshape(-1, channels)
        back.append(exchange(x))
    result = None
    for f in range(frame_count):
        result = restore_call(f, back[f], order_back, frames.shape, result)
    return result


def solution(mesh):
    in_specs = (P(None, "ha", "wa", None), P(), P(), P(), P(), P(), P(), P(), P(), P())
    out_specs = P(None, "ha", "wa", None)
    return jax.shard_map(body, mesh=mesh, in_specs=in_specs, out_specs=out_specs, check_vma=False)
```

```python
import math

import jax
import jax.numpy as jnp
import numpy as np
from jax import lax
from jax.experimental import pallas as pl
from jax.experimental.pallas import tpu as pltpu
from jax.sharding import PartitionSpec as P

HEADS = 12
GRID = 16
SEG = 8
CHUNK = 1536
F32 = jnp.float32
BF16 = jnp.bfloat16
MIB = 1024 * 1024


def gelu(v):
    cubic = v * (math.sqrt(2 / math.pi) + (math.sqrt(2 / math.pi) * 0.044715) * (v * v))
    half = 0.5 * v
    return half + half * jnp.tanh(cubic)


def half_gelu(h):
    root = math.sqrt(2 / math.pi)
    return h + h * jnp.tanh(h * (2 * root + (8 * root * 0.044715) * (h * h)))


def normalize(values):
    mean_val = jnp.mean(values, axis=-1, keepdims=True)
    centred = values - mean_val
    variance = jnp.mean(centred * centred, axis=-1, keepdims=True)
    return centred * lax.rsqrt(variance + 1e-05)


def dot(a, b):
    return jnp.dot(a, b, preferred_element_type=F32)


def dot_t(a, b):
    return lax.dot_general(a, b, (((1,), (1,)), ((), ())), preferred_element_type=F32)


def segment_order(cols, count):
    steps = cols // SEG
    matrix = np.zeros((count * cols, count * cols), np.float32)
    for row in range(count):
        for t in range(steps):
            for s in range(SEG):
                matrix[row * cols + t * SEG + s, row * cols + s * steps + t] = 1
    return matrix


def segments(cols, count):
    steps = cols // SEG
    shape = (count * cols, count * cols)
    place = lax.broadcasted_iota(jnp.int32, shape, 0)
    inside = place % cols
    source = place - inside + inside % SEG * steps + inside // SEG
    return jnp.where(lax.broadcasted_iota(jnp.int32, shape, 1) == source, 0.5, 0.0).astype(BF16)


def message_order(row_groups, cols, col_stride, cols_each):
    col_groups = cols // col_stride
    dests = col_stride // cols_each
    matrix = np.zeros((row_groups * cols, row_groups * cols), np.float32)
    place = 0
    for w in range(dests):
        for b in range(cols_each):
            for g in range(row_groups):
                for h in range(col_groups):
                    matrix[place, g * cols + h * col_stride + w * cols_each + b] = 1
                    place += 1
    return matrix


def expand_kernel(frame, x_ref, expand_ref, expanded, tokens):
    rows, steps, _, hidden = expanded.shape
    cols = steps * SEG
    channels = x_ref.shape[-1]
    pair = 2 * cols
    seg = segments(cols, 2)
    for r in range(rows // 2):
        both = x_ref[frame, 2 * r : 2 * r + 2].reshape(pair, channels)
        tokens[r * pair : (r + 1) * pair] = dot(seg, both).astype(BF16)
    block = 4
    for c in range(hidden // CHUNK):
        lanes = slice(c * CHUNK, (c + 1) * CHUNK)
        for r in range(0, rows, block):
            value = half_gelu(dot(tokens[r * cols : (r + block) * cols], expand_ref[:, lanes]))
            expanded[r : r + block, :, :, lanes] = value.reshape(block, steps, SEG, CHUNK)


def expand_call(frame, x, expand_weight):
    _, rows, cols, channels = x.shape
    hidden = expand_weight.shape[1]

    def body(*refs):
        expand_kernel(frame, *refs)

    return pl.pallas_call(
        body,
        in_specs=[pl.BlockSpec(memory_space=pltpu.VMEM)] * 2,
        out_specs=[pl.BlockSpec(memory_space=pltpu.VMEM)] * 2,
        out_shape=[
            jax.ShapeDtypeStruct((rows, cols // SEG, SEG, hidden), F32),
            jax.ShapeDtypeStruct((rows * cols, channels), BF16),
        ],
        compiler_params=pltpu.CompilerParams(vmem_limit_bytes=24 * MIB),
        cost_estimate=pl.CostEstimate(flops=3 * 10**9, bytes_accessed=4 * 10**6, transcendentals=2 * 10**6),
    )(x, expand_weight)


def conv_kernel(
    frame,
    keep_ref,
    even_ref,
    own_ref,
    tokens,
    expand_ref,
    dw_any,
    bias_any,
    order_any,
    outer_rows_any,
    inner_rows_any,
    outer_cols_any,
    inner_cols_any,
    project_any,
    out_ref,
    dw_ref,
    bias_ref,
    order_ref,
    outer_rows,
    inner_rows,
    outer_cols,
    inner_cols,
    project_ref,
    sems,
    sides,
    side_vals,
    taps,
    edge_cols,
    edge_rows,
    mixed,
    total,
):
    rows, steps, _, hidden = own_ref.shape
    cols = steps * SEG
    pairs = [
        (outer_rows_any.at[frame], outer_rows),
        (inner_rows_any.at[frame], inner_rows),
        (outer_cols_any.at[frame], outer_cols),
        (inner_cols_any.at[frame], inner_cols),
        (dw_any, dw_ref),
        (bias_any, bias_ref),
        (project_any, project_ref),
        (order_any, order_ref),
    ]
    copies = [pltpu.make_async_copy(src, dst, sems.at[i]) for i, (src, dst) in enumerate(pairs)]
    for copy in copies:
        copy.start()
    sides[...] = jnp.zeros_like(sides)
    for copy in copies[0:4]:
        copy.wait()
    even_row, even_col = even_ref[0] == 1, even_ref[1] == 1
    outer, inner = outer_rows[...], inner_rows[...]
    top, bottom = jnp.where(even_row, outer, inner), jnp.where(even_row, inner, outer)
    outer, inner = outer_cols[...], inner_cols[...]
    left, right = jnp.where(even_col, outer, inner), jnp.where(even_col, inner, outer)
    seg_one = segments(cols, 1)
    top_tokens = dot(seg_one, top[0:cols]).astype(BF16)
    bottom_tokens = dot(seg_one, bottom[0:cols]).astype(BF16)
    top = 0.5 * top[cols : cols + 16].astype(F32)
    bottom = 0.5 * bottom[cols : cols + 16].astype(F32)
    sides[0:1] = top[0:1]
    sides[1 : rows + 1] = 0.5 * left.astype(F32)
    sides[rows + 1 : rows + 2] = bottom[0:1]
    sides[24:25] = top[1:2]
    sides[25 : rows + 25] = 0.5 * right.astype(F32)
    sides[rows + 25 : rows + 26] = bottom[1:2]
    halo = jnp.concatenate([top_tokens, bottom_tokens, sides[...].astype(BF16)], axis=0)
    place = lax.broadcasted_iota(jnp.int32, (SEG, CHUNK), 0)
    for copy in copies[4:6]:
        copy.wait()
    for i in range(3):
        taps[3 * i : 3 * i + 3] = 0.5 * dw_ref[i]
    taps[9:10] = 0.5 * bias_ref[...].reshape(1, hidden)

    def expand_halo(c):
        lanes = slice(c * CHUNK, (c + 1) * CHUNK)
        value = half_gelu(dot(halo, expand_ref[:, lanes]))
        edge_rows[:, :, :, lanes] = value[: 2 * cols].reshape(2, steps, SEG, CHUNK)
        side_vals[:, lanes] = value[2 * cols :]

    def plain(r, t, lanes):
        if r == 0:
            return edge_rows[0, t, :, lanes]
        if r == rows + 1:
            return edge_rows[1, t, :, lanes]
        return own_ref[r - 1, t, :, lanes]

    def fill_edges(c, r):
        lanes = slice(c * CHUNK, (c + 1) * CHUNK)
        before = pltpu.roll(plain(r, steps - 1, lanes), 1, 0)
        edge_cols[r, 0, :, lanes] = jnp.where(place == 0, side_vals[r : r + 1, lanes], before)
        after = pltpu.roll(plain(r, 0, lanes), SEG - 1, 0)
        edge_cols[r, 1, :, lanes] = jnp.where(place == SEG - 1, side_vals[24 + r : 25 + r, lanes], after)

    def conv_row(c, r):
        pieces = []
        for lt in range(CHUNK // 128):
            lanes = slice(c * CHUNK + lt * 128, c * CHUNK + (lt + 1) * 128)
            acc = jnp.broadcast_to(taps[9:10, lanes].reshape(1, 1, 128), (steps, SEG, 128))
            for i in range(3):
                if r + i == 0:
                    middle = edge_rows[0, :, :, lanes]
                elif r + i == rows + 1:
                    middle = edge_rows[1, :, :, lanes]
                else:
                    middle = own_ref[r + i - 1, :, :, lanes]
                window = jnp.concatenate(
                    [edge_cols[r + i, 0:1, :, lanes], middle, edge_cols[r + i, 1:2, :, lanes]], axis=0
                )
                for j in range(3):
                    acc = acc + window[j : j + steps] * taps[3 * i + j : 3 * i + j + 1, lanes].reshape(1, 1, 128)
            pieces.append(half_gelu(acc).reshape(cols, 128).astype(BF16))
        return jnp.concatenate(pieces, axis=1)

    def project_rows(c, start, stop, values):
        lanes = slice(c * CHUNK, (c + 1) * CHUNK)
        span = slice(start * cols, stop * cols)
        branch = dot(jnp.concatenate(values, axis=0), project_ref[lanes])
        total[span] = branch if c == 0 else total[span] + branch

    part = rows // 2
    for c in range(hidden // CHUNK):
        expand_halo(c)
        if c == 0:
            copies[6].wait()
            copies[7].wait()
        fill_edges(c, 0)
        fill_edges(c, 1)
        values, ready = [], None
        for r in range(rows):
            fill_edges(c, r + 2)
            values.append(conv_row(c, r))
            if len(values) == part:
                if ready is not None:
                    project_rows(c, r + 1 - 2 * part, r + 1 - part, ready)
                ready, values = values, []
        project_rows(c, rows - part, rows, ready)

    flag = keep_ref[frame, 0].astype(F32)
    span = order_ref.shape[0]
    groups = span // cols
    stride = rows // groups
    order = order_ref[...]
    for d in range(stride):
        parts = []
        for g in range(groups):
            r = g * stride + d
            residual = 2.0 * tokens[r * cols : (r + 1) * cols].astype(F32)
            parts.append((residual + flag * total[r * cols : (r + 1) * cols]).astype(BF16))
        value = parts[0] if groups == 1 else jnp.concatenate(parts, axis=0)
        out_ref[d * span : (d + 1) * span] = dot(order, value).astype(BF16)


def conv_call(frame, keep, even, own, tokens, expand_weight, dw, bias, order, halo, project_weight):
    rows, steps, _, hidden = own.shape
    cols = steps * SEG
    channels = tokens.shape[1]
    large = [dw, bias, order, *halo, project_weight]

    def body(*refs):
        conv_kernel(frame, *refs)

    def buffer(a, k):
        return pltpu.VMEM(a.shape[1:] if 3 <= k < 7 else a.shape, a.dtype)

    return pl.pallas_call(
        body,
        in_specs=[pl.BlockSpec(memory_space=pltpu.SMEM)] * 2
        + [pl.BlockSpec(memory_space=pltpu.VMEM)] * 3
        + [pl.BlockSpec(memory_space=pl.ANY)] * len(large),
        out_specs=pl.BlockSpec(memory_space=pltpu.VMEM),
        out_shape=jax.ShapeDtypeStruct((rows * cols, channels), BF16),
        scratch_shapes=[buffer(a, k) for k, a in enumerate(large)]
        + [
            pltpu.SemaphoreType.DMA((len(large),)),
            pltpu.VMEM((48, channels), F32),
            pltpu.VMEM((48, hidden), F32),
            pltpu.VMEM((16, hidden), F32),
            pltpu.VMEM((rows + 2, 2, SEG, hidden), F32),
            pltpu.VMEM((2, steps, SEG, hidden), F32),
            pltpu.VMEM((rows * cols, hidden), BF16),
            pltpu.VMEM((rows * cols, channels), F32),
        ],
        compiler_params=pltpu.CompilerParams(vmem_limit_bytes=32 * MIB),
        cost_estimate=pl.CostEstimate(flops=4 * 10**9, bytes_accessed=4 * 10**6, transcendentals=2 * 10**6),
    )(keep, even, own, tokens, expand_weight, *large)


def window_kernel(frame, keep_ref, x_ref, qkv_ref, out_w_ref, in_ref, down_ref, out_ref, held):
    windows = held.shape[1]
    sources, _, group, channels = held.shape
    count = sources * group
    head_dim = channels // HEADS
    per_tile = 128 // head_dim
    scale = head_dim ** (-0.5) * math.log2(math.e)
    held[...] = x_ref[...].astype(F32).reshape(held.shape)
    attend_flag = keep_ref[frame, 1].astype(F32)
    mlp_flag = keep_ref[frame, 2].astype(F32)
    head_of_lane = lax.broadcasted_iota(jnp.int32, (1, 128), 1) // head_dim
    ones = jnp.ones((count, 128), BF16)
    none = jnp.zeros((), BF16)

    def attend(residual):
        qkv = dot(normalize(residual).astype(BF16), qkv_ref[...]).astype(BF16)
        tiles = []
        for t in range(channels // 128):
            queries = qkv[:, t * 128 : (t + 1) * 128]
            keys_part = qkv[:, channels + t * 128 : channels + (t + 1) * 128]
            values_part = qkv[:, 2 * channels + t * 128 : 2 * channels + (t + 1) * 128]
            values_part = jnp.concatenate([values_part, ones], axis=1)
            tile = None
            for i in range(per_tile):
                scores = dot_t(jnp.where(head_of_lane == i, queries, none), keys_part)
                top_score = jnp.max(scores, axis=1, keepdims=True)
                weights = jnp.exp2((scores - top_score) * scale).astype(BF16)
                both = dot(weights, values_part)
                share = both[:, :128] * (1.0 / both[:, 128:])
                tile = share if tile is None else jnp.where(head_of_lane == i, share, tile)
            tiles.append(tile.astype(BF16))
        update = dot(jnp.concatenate(tiles, axis=1), out_w_ref[...])
        return (residual + attend_flag * update).astype(BF16).astype(F32)

    def mlp(residual):
        inner = gelu(dot(normalize(residual).astype(BF16), in_ref[...])).astype(BF16)
        return residual + mlp_flag * dot(inner, down_ref[...])

    def one_window(w, _):
        second = attend(held[:, w].reshape(count, channels))
        held[:, w] = mlp(second).reshape(sources, group, channels)
        return 0

    lax.fori_loop(0, windows, one_window, 0)
    out_ref[...] = held[...].reshape(out_ref.shape).astype(BF16)


def window_call(frame, keep, x, windows, group, qkv_weight, out_weight, mlp_in, mlp_out):
    tokens, channels = x.shape
    held = (tokens // (windows * group), windows, group, channels)

    def body(*refs):
        window_kernel(frame, *refs)

    return pl.pallas_call(
        body,
        in_specs=[pl.BlockSpec(memory_space=pltpu.SMEM)] + [pl.BlockSpec(memory_space=pltpu.VMEM)] * 5,
        out_specs=pl.BlockSpec(memory_space=pltpu.VMEM),
        out_shape=jax.ShapeDtypeStruct(x.shape, BF16),
        scratch_shapes=[pltpu.VMEM(held, F32)],
        compiler_params=pltpu.CompilerParams(vmem_limit_bytes=40 * MIB),
        cost_estimate=pl.CostEstimate(flops=9 * 10**9, bytes_accessed=4 * 10**6, transcendentals=6 * 10**6),
    )(keep, x, qkv_weight, out_weight, mlp_in, mlp_out)


def restore_kernel(x_ref, order_ref, *rest):
    out_ref = rest[-1]
    _, rows, cols, channels = out_ref.shape
    span = order_ref.shape[0]
    groups = span // cols
    stride = rows // groups
    order = order_ref[...]
    for d in range(stride):
        back = dot(order, x_ref[d * span : (d + 1) * span]).astype(BF16)
        for g in range(groups):
            out_ref[0, g * stride + d] = back[g * cols : (g + 1) * cols]


def restore_call(frame, x, order, out_shape, previous):
    _, rows, cols, channels = out_shape

    def whole(a):
        return pl.BlockSpec(a.shape, lambda i, n=a.ndim: (0,) * n)

    args = [x, order]
    specs = [whole(a) for a in args]
    aliases = {}
    if previous is not None:
        aliases = {len(args): 0}
        args.append(previous)
        specs.append(pl.BlockSpec(memory_space=pl.ANY))
    return pl.pallas_call(
        restore_kernel,
        grid=(1,),
        in_specs=specs,
        out_specs=pl.BlockSpec((1, rows, cols, channels), lambda i: (frame, 0, 0, 0)),
        out_shape=jax.ShapeDtypeStruct(out_shape, BF16),
        input_output_aliases=aliases,
        compiler_params=pltpu.CompilerParams(vmem_limit_bytes=16 * MIB),
        cost_estimate=pl.CostEstimate(flops=10**8, bytes_accessed=2 * 10**6, transcendentals=0),
    )(*args)


def neighbours(first, last, axis):
    size = lax.axis_size(axis)
    even = lax.axis_index(axis) % 2 == 0
    inner = [(i, i ^ 1) for i in range(size)]
    outer = [(i, i + 1) for i in range(1, size - 1, 2)]
    outer = outer + [(j, i) for i, j in outer]
    across = lax.ppermute(jnp.where(even, first, last), axis, outer)
    within = lax.ppermute(jnp.where(even, last, first), axis, inner)
    return even, across, within


def body(
    frames,
    keep,
    expand_weight,
    dw_kernel,
    conv_bias,
    project_weight,
    qkv_weight,
    out_weight,
    mlp_in,
    mlp_out,
):
    frame_count, rows, cols, channels = frames.shape
    rows_axis = lax.axis_size("ha")
    cols_axis = lax.axis_size("wa")
    row_stride = rows * rows_axis // GRID
    col_stride = cols * cols_axis // GRID
    assert row_stride == rows_axis and col_stride % cols_axis == 0
    cols_each = col_stride // cols_axis
    row_groups = rows // row_stride
    col_groups = cols // col_stride
    group = row_groups * col_groups
    devices = rows_axis * cols_axis

    even_col, outer_cols, inner_cols = neighbours(frames[:, :, 0], frames[:, :, cols - 1], "wa")
    left = jnp.where(even_col, outer_cols, inner_cols)
    right = jnp.where(even_col, inner_cols, outer_cols)

    def edge(r):
        spare = jnp.zeros((frame_count, 14, channels), BF16)
        return jnp.concatenate([frames[:, r], left[:, r : r + 1], right[:, r : r + 1], spare], axis=1)

    even_row, outer_rows, inner_rows = neighbours(edge(0), edge(rows - 1), "ha")
    halo = (outer_rows, inner_rows, outer_cols, inner_cols)
    even = jnp.stack([even_row, even_col]).astype(jnp.int32)

    to_message = message_order(row_groups, cols, col_stride, cols_each)
    from_segments = np.kron(np.eye(row_groups), segment_order(cols, 1)).T
    order = jnp.asarray(to_message @ from_segments, BF16)
    order_back = jnp.asarray(to_message.T, BF16)
    def exchange(x):
        message = x.reshape(devices, -1, channels)
        return lax.all_to_all(message, ("ha", "wa"), split_axis=0, concat_axis=0, tiled=True).reshape(-1, channels)

    sent = []
    for f in range(frame_count):
        own, tokens = expand_call(f, frames, expand_weight)
        first = conv_call(
            f, keep, even, own, tokens, expand_weight, dw_kernel, conv_bias, order, halo, project_weight
        )
        sent.append(exchange(first))
    back = []
    for f in range(frame_count):
        x = sent[f]
        if group != 8:
            x = x.reshape(devices, cols_each, group, channels).swapaxes(0, 1).reshape(cols_each, -1, 8, channels)
            x = x.swapaxes(0, 1).reshape(-1, channels)
        x = window_call(f, keep, x, cols_each, 8, qkv_weight, out_weight, mlp_in, mlp_out)
        if group != 8:
            x = x.reshape(-1, cols_each, 8, channels).swapaxes(0, 1).reshape(cols_each, devices, group, channels)
            x = x.swapaxes(0, 1).reshape(-1, channels)
        back.append(exchange(x))
    result = None
    for f in range(frame_count):
        result = restore_call(f, back[f], order_back, frames.shape, result)
    return result


def solution(mesh):
    in_specs = (P(None, "ha", "wa", None), P(), P(), P(), P(), P(), P(), P(), P(), P())
    out_specs = P(None, "ha", "wa", None)
    return jax.shard_map(body, mesh=mesh, in_specs=in_specs, out_specs=out_specs, check_vma=False)
```

```python
import math

import jax
import jax.numpy as jnp
import numpy as np
from jax import lax
from jax.experimental import pallas as pl
from jax.experimental.pallas import tpu as pltpu
from jax.sharding import PartitionSpec as P

HEADS = 12
GRID = 16
SEG = 8
CHUNK = 1536
F32 = jnp.float32
BF16 = jnp.bfloat16
MIB = 1024 * 1024


def gelu(v):
    cubic = v * (math.sqrt(2 / math.pi) + (math.sqrt(2 / math.pi) * 0.044715) * (v * v))
    half = 0.5 * v
    return half + half * jnp.tanh(cubic)


def half_gelu(h):
    root = math.sqrt(2 / math.pi)
    return h + h * jnp.tanh(h * (2 * root + (8 * root * 0.044715) * (h * h)))


def normalize(values):
    mean_val = jnp.mean(values, axis=-1, keepdims=True)
    centred = values - mean_val
    variance = jnp.mean(centred * centred, axis=-1, keepdims=True)
    return centred * lax.rsqrt(variance + 1e-05)


def dot(a, b):
    return jnp.dot(a, b, preferred_element_type=F32)


def dot_t(a, b):
    return lax.dot_general(a, b, (((1,), (1,)), ((), ())), preferred_element_type=F32)


def segment_order(cols, count):
    steps = cols // SEG
    matrix = np.zeros((count * cols, count * cols), np.float32)
    for row in range(count):
        for t in range(steps):
            for s in range(SEG):
                matrix[row * cols + t * SEG + s, row * cols + s * steps + t] = 1
    return matrix


def segments(cols, count):
    steps = cols // SEG
    shape = (count * cols, count * cols)
    place = lax.broadcasted_iota(jnp.int32, shape, 0)
    inside = place % cols
    source = place - inside + inside % SEG * steps + inside // SEG
    return jnp.where(lax.broadcasted_iota(jnp.int32, shape, 1) == source, 0.5, 0.0).astype(BF16)


def message_order(row_groups, cols, col_stride, cols_each):
    col_groups = cols // col_stride
    dests = col_stride // cols_each
    matrix = np.zeros((row_groups * cols, row_groups * cols), np.float32)
    place = 0
    for w in range(dests):
        for b in range(cols_each):
            for g in range(row_groups):
                for h in range(col_groups):
                    matrix[place, g * cols + h * col_stride + w * cols_each + b] = 1
                    place += 1
    return matrix


def expand_kernel(frame, x_ref, expand_ref, expanded, tokens):
    rows, steps, _, hidden = expanded.shape
    cols = steps * SEG
    channels = x_ref.shape[-1]
    pair = 2 * cols
    seg = segments(cols, 2)
    for r in range(rows // 2):
        both = x_ref[frame, 2 * r : 2 * r + 2].reshape(pair, channels)
        tokens[r * pair : (r + 1) * pair] = dot(seg, both).astype(BF16)
    block = 4
    for c in range(hidden // CHUNK):
        lanes = slice(c * CHUNK, (c + 1) * CHUNK)
        for r in range(0, rows, block):
            value = half_gelu(dot(tokens[r * cols : (r + block) * cols], expand_ref[:, lanes]))
            expanded[r : r + block, :, :, lanes] = value.reshape(block, steps, SEG, CHUNK)


def expand_call(frame, x, expand_weight):
    _, rows, cols, channels = x.shape
    hidden = expand_weight.shape[1]

    def body(*refs):
        expand_kernel(frame, *refs)

    return pl.pallas_call(
        body,
        in_specs=[pl.BlockSpec(memory_space=pltpu.VMEM)] * 2,
        out_specs=[pl.BlockSpec(memory_space=pltpu.VMEM)] * 2,
        out_shape=[
            jax.ShapeDtypeStruct((rows, cols // SEG, SEG, hidden), F32),
            jax.ShapeDtypeStruct((rows * cols, channels), BF16),
        ],
        compiler_params=pltpu.CompilerParams(vmem_limit_bytes=24 * MIB),
        cost_estimate=pl.CostEstimate(flops=3 * 10**9, bytes_accessed=4 * 10**6, transcendentals=2 * 10**6),
    )(x, expand_weight)


def conv_kernel(
    frame,
    keep_ref,
    even_ref,
    own_ref,
    tokens,
    expand_ref,
    dw_any,
    bias_any,
    order_any,
    outer_rows_any,
    inner_rows_any,
    outer_cols_any,
    inner_cols_any,
    project_any,
    out_ref,
    dw_ref,
    bias_ref,
    order_ref,
    outer_rows,
    inner_rows,
    outer_cols,
    inner_cols,
    project_ref,
    sems,
    sides,
    side_vals,
    taps,
    edge_cols,
    edge_rows,
    mixed,
    total,
):
    rows, steps, _, hidden = own_ref.shape
    cols = steps * SEG
    pairs = [
        (outer_rows_any.at[frame], outer_rows),
        (inner_rows_any.at[frame], inner_rows),
        (outer_cols_any.at[frame], outer_cols),
        (inner_cols_any.at[frame], inner_cols),
        (dw_any, dw_ref),
        (bias_any, bias_ref),
        (project_any, project_ref),
        (order_any, order_ref),
    ]
    copies = [pltpu.make_async_copy(src, dst, sems.at[i]) for i, (src, dst) in enumerate(pairs)]
    for copy in copies:
        copy.start()
    sides[...] = jnp.zeros_like(sides)
    for copy in copies[0:4]:
        copy.wait()
    even_row, even_col = even_ref[0] == 1, even_ref[1] == 1
    outer, inner = outer_rows[...], inner_rows[...]
    top, bottom = jnp.where(even_row, outer, inner), jnp.where(even_row, inner, outer)
    outer, inner = outer_cols[...], inner_cols[...]
    left, right = jnp.where(even_col, outer, inner), jnp.where(even_col, inner, outer)
    seg_one = segments(cols, 1)
    top_tokens = dot(seg_one, top[0:cols]).astype(BF16)
    bottom_tokens = dot(seg_one, bottom[0:cols]).astype(BF16)
    top = 0.5 * top[cols : cols + 16].astype(F32)
    bottom = 0.5 * bottom[cols : cols + 16].astype(F32)
    sides[0:1] = top[0:1]
    sides[1 : rows + 1] = 0.5 * left.astype(F32)
    sides[rows + 1 : rows + 2] = bottom[0:1]
    sides[24:25] = top[1:2]
    sides[25 : rows + 25] = 0.5 * right.astype(F32)
    sides[rows + 25 : rows + 26] = bottom[1:2]
    halo = jnp.concatenate([top_tokens, bottom_tokens, sides[...].astype(BF16)], axis=0)
    place = lax.broadcasted_iota(jnp.int32, (SEG, CHUNK), 0)
    for copy in copies[4:6]:
        copy.wait()
    outside = 0.25 * (dw_ref[0] + dw_ref[2])
    centre = 0.25 * dw_ref[1]
    taps[0:3] = 0.5 * dw_ref[0]
    taps[3:6] = outside + centre
    taps[6:9] = outside - centre
    taps[9:12] = 0.5 * dw_ref[2]
    taps[12:13] = 0.5 * bias_ref[...].reshape(1, hidden)

    def expand_halo(c):
        lanes = slice(c * CHUNK, (c + 1) * CHUNK)
        value = half_gelu(dot(halo, expand_ref[:, lanes]))
        edge_rows[:, :, :, lanes] = value[: 2 * cols].reshape(2, steps, SEG, CHUNK)
        side_vals[:, lanes] = value[2 * cols :]

    def plain(r, t, lanes):
        if r == 0:
            return edge_rows[0, t, :, lanes]
        if r == rows + 1:
            return edge_rows[1, t, :, lanes]
        return own_ref[r - 1, t, :, lanes]

    def fill_edges(c, r):
        lanes = slice(c * CHUNK, (c + 1) * CHUNK)
        before = pltpu.roll(plain(r, steps - 1, lanes), 1, 0)
        edge_cols[r, 0, :, lanes] = jnp.where(place == 0, side_vals[r : r + 1, lanes], before)
        after = pltpu.roll(plain(r, 0, lanes), SEG - 1, 0)
        edge_cols[r, 1, :, lanes] = jnp.where(place == SEG - 1, side_vals[24 + r : 25 + r, lanes], after)

    def line(r, lanes):
        if r == 0:
            middle = edge_rows[0, :, :, lanes]
        elif r == rows + 1:
            middle = edge_rows[1, :, :, lanes]
        else:
            middle = own_ref[r - 1, :, :, lanes]
        return jnp.concatenate([edge_cols[r, 0:1, :, lanes], middle, edge_cols[r, 1:2, :, lanes]], axis=0)

    def conv_pair(c, r):
        upper, lower = [], []
        for lt in range(CHUNK // 128):
            lanes = slice(c * CHUNK + lt * 128, c * CHUNK + (lt + 1) * 128)
            d = [line(r + k, lanes) for k in range(4)]
            mixes = [d[0] - d[2], d[1] + d[2], d[2] - d[1], d[1] - d[3]]
            products = []
            for k in range(4):
                acc = jnp.broadcast_to(taps[12:13, lanes].reshape(1, 1, 128), (steps, SEG, 128)) if k == 1 else None
                for j in range(3):
                    term = mixes[k][j : j + steps] * taps[3 * k + j : 3 * k + j + 1, lanes].reshape(1, 1, 128)
                    acc = term if acc is None else acc + term
                products.append(acc)
            first = products[0] + products[1] + products[2]
            second = products[1] - products[2] - products[3]
            upper.append(half_gelu(first).reshape(cols, 128).astype(BF16))
            lower.append(half_gelu(second).reshape(cols, 128).astype(BF16))
        return jnp.concatenate([jnp.concatenate(upper, axis=1), jnp.concatenate(lower, axis=1)], axis=0)

    def project_rows(c, start, stop, values):
        lanes = slice(c * CHUNK, (c + 1) * CHUNK)
        span = slice(start * cols, stop * cols)
        branch = dot(jnp.concatenate(values, axis=0), project_ref[lanes])
        total[span] = branch if c == 0 else total[span] + branch

    part = rows // 2
    for c in range(hidden // CHUNK):
        expand_halo(c)
        if c == 0:
            copies[6].wait()
            copies[7].wait()
        fill_edges(c, 0)
        fill_edges(c, 1)
        values, ready = [], None
        for r in range(rows):
            fill_edges(c, r + 2)
            if r % 2 == 1:
                values.append(conv_pair(c, r - 1))
            if 2 * len(values) == part:
                if ready is not None:
                    project_rows(c, r + 1 - 2 * part, r + 1 - part, ready)
                ready, values = values, []
        project_rows(c, rows - part, rows, ready)

    flag = keep_ref[frame, 0].astype(F32)
    span = order_ref.shape[0]
    groups = span // cols
    stride = rows // groups
    order = order_ref[...]
    for d in range(stride):
        parts = []
        for g in range(groups):
            r = g * stride + d
            residual = 2.0 * tokens[r * cols : (r + 1) * cols].astype(F32)
            parts.append((residual + flag * total[r * cols : (r + 1) * cols]).astype(BF16))
        value = parts[0] if groups == 1 else jnp.concatenate(parts, axis=0)
        out_ref[d * span : (d + 1) * span] = dot(order, value).astype(BF16)


def conv_call(frame, keep, even, own, tokens, expand_weight, dw, bias, order, halo, project_weight):
    rows, steps, _, hidden = own.shape
    cols = steps * SEG
    channels = tokens.shape[1]
    large = [dw, bias, order, *halo, project_weight]

    def body(*refs):
        conv_kernel(frame, *refs)

    def buffer(a, k):
        return pltpu.VMEM(a.shape[1:] if 3 <= k < 7 else a.shape, a.dtype)

    return pl.pallas_call(
        body,
        in_specs=[pl.BlockSpec(memory_space=pltpu.SMEM)] * 2
        + [pl.BlockSpec(memory_space=pltpu.VMEM)] * 3
        + [pl.BlockSpec(memory_space=pl.ANY)] * len(large),
        out_specs=pl.BlockSpec(memory_space=pltpu.VMEM),
        out_shape=jax.ShapeDtypeStruct((rows * cols, channels), BF16),
        scratch_shapes=[buffer(a, k) for k, a in enumerate(large)]
        + [
            pltpu.SemaphoreType.DMA((len(large),)),
            pltpu.VMEM((48, channels), F32),
            pltpu.VMEM((48, hidden), F32),
            pltpu.VMEM((16, hidden), F32),
            pltpu.VMEM((rows + 2, 2, SEG, hidden), F32),
            pltpu.VMEM((2, steps, SEG, hidden), F32),
            pltpu.VMEM((rows * cols, hidden), BF16),
            pltpu.VMEM((rows * cols, channels), F32),
        ],
        compiler_params=pltpu.CompilerParams(vmem_limit_bytes=32 * MIB),
        cost_estimate=pl.CostEstimate(flops=4 * 10**9, bytes_accessed=4 * 10**6, transcendentals=2 * 10**6),
    )(keep, even, own, tokens, expand_weight, *large)


def window_kernel(frame, keep_ref, x_ref, qkv_ref, out_w_ref, in_ref, down_ref, out_ref, held):
    windows = held.shape[1]
    sources, _, group, channels = held.shape
    count = sources * group
    head_dim = channels // HEADS
    per_tile = 128 // head_dim
    scale = head_dim ** (-0.5) * math.log2(math.e)
    held[...] = x_ref[...].astype(F32).reshape(held.shape)
    attend_flag = keep_ref[frame, 1].astype(F32)
    mlp_flag = keep_ref[frame, 2].astype(F32)
    head_of_lane = lax.broadcasted_iota(jnp.int32, (1, 128), 1) // head_dim
    ones = jnp.ones((count, 128), BF16)
    none = jnp.zeros((), BF16)

    def attend(residual):
        qkv = dot(normalize(residual).astype(BF16), qkv_ref[...]).astype(BF16)
        tiles = []
        for t in range(channels // 128):
            queries = qkv[:, t * 128 : (t + 1) * 128]
            keys_part = qkv[:, channels + t * 128 : channels + (t + 1) * 128]
            values_part = qkv[:, 2 * channels + t * 128 : 2 * channels + (t + 1) * 128]
            values_part = jnp.concatenate([values_part, ones], axis=1)
            tile = None
            for i in range(per_tile):
                scores = dot_t(jnp.where(head_of_lane == i, queries, none), keys_part)
                top_score = jnp.max(scores, axis=1, keepdims=True)
                weights = jnp.exp2((scores - top_score) * scale).astype(BF16)
                both = dot(weights, values_part)
                share = both[:, :128] * (1.0 / both[:, 128:])
                tile = share if tile is None else jnp.where(head_of_lane == i, share, tile)
            tiles.append(tile.astype(BF16))
        update = dot(jnp.concatenate(tiles, axis=1), out_w_ref[...])
        return (residual + attend_flag * update).astype(BF16).astype(F32)

    def mlp(residual):
        inner = gelu(dot(normalize(residual).astype(BF16), in_ref[...])).astype(BF16)
        return residual + mlp_flag * dot(inner, down_ref[...])

    def one_window(w, _):
        second = attend(held[:, w].reshape(count, channels))
        held[:, w] = mlp(second).reshape(sources, group, channels)
        return 0

    lax.fori_loop(0, windows, one_window, 0)
    out_ref[...] = held[...].reshape(out_ref.shape).astype(BF16)


def window_call(frame, keep, x, windows, group, qkv_weight, out_weight, mlp_in, mlp_out):
    tokens, channels = x.shape
    held = (tokens // (windows * group), windows, group, channels)

    def body(*refs):
        window_kernel(frame, *refs)

    return pl.pallas_call(
        body,
        in_specs=[pl.BlockSpec(memory_space=pltpu.SMEM)] + [pl.BlockSpec(memory_space=pltpu.VMEM)] * 5,
        out_specs=pl.BlockSpec(memory_space=pltpu.VMEM),
        out_shape=jax.ShapeDtypeStruct(x.shape, BF16),
        scratch_shapes=[pltpu.VMEM(held, F32)],
        compiler_params=pltpu.CompilerParams(vmem_limit_bytes=40 * MIB),
        cost_estimate=pl.CostEstimate(flops=9 * 10**9, bytes_accessed=4 * 10**6, transcendentals=6 * 10**6),
    )(keep, x, qkv_weight, out_weight, mlp_in, mlp_out)


def restore_kernel(x_ref, order_ref, *rest):
    out_ref = rest[-1]
    _, rows, cols, channels = out_ref.shape
    span = order_ref.shape[0]
    groups = span // cols
    stride = rows // groups
    order = order_ref[...]
    for d in range(stride):
        back = dot(order, x_ref[d * span : (d + 1) * span]).astype(BF16)
        for g in range(groups):
            out_ref[0, g * stride + d] = back[g * cols : (g + 1) * cols]


def restore_call(frame, x, order, out_shape, previous):
    _, rows, cols, channels = out_shape

    def whole(a):
        return pl.BlockSpec(a.shape, lambda i, n=a.ndim: (0,) * n)

    args = [x, order]
    specs = [whole(a) for a in args]
    aliases = {}
    if previous is not None:
        aliases = {len(args): 0}
        args.append(previous)
        specs.append(pl.BlockSpec(memory_space=pl.ANY))
    return pl.pallas_call(
        restore_kernel,
        grid=(1,),
        in_specs=specs,
        out_specs=pl.BlockSpec((1, rows, cols, channels), lambda i: (frame, 0, 0, 0)),
        out_shape=jax.ShapeDtypeStruct(out_shape, BF16),
        input_output_aliases=aliases,
        compiler_params=pltpu.CompilerParams(vmem_limit_bytes=16 * MIB),
        cost_estimate=pl.CostEstimate(flops=10**8, bytes_accessed=2 * 10**6, transcendentals=0),
    )(*args)


def neighbours(first, last, axis):
    size = lax.axis_size(axis)
    even = lax.axis_index(axis) % 2 == 0
    inner = [(i, i ^ 1) for i in range(size)]
    outer = [(i, i + 1) for i in range(1, size - 1, 2)]
    outer = outer + [(j, i) for i, j in outer]
    across = lax.ppermute(jnp.where(even, first, last), axis, outer)
    within = lax.ppermute(jnp.where(even, last, first), axis, inner)
    return even, across, within


def body(
    frames,
    keep,
    expand_weight,
    dw_kernel,
    conv_bias,
    project_weight,
    qkv_weight,
    out_weight,
    mlp_in,
    mlp_out,
):
    frame_count, rows, cols, channels = frames.shape
    rows_axis = lax.axis_size("ha")
    cols_axis = lax.axis_size("wa")
    row_stride = rows * rows_axis // GRID
    col_stride = cols * cols_axis // GRID
    assert row_stride == rows_axis and col_stride % cols_axis == 0
    cols_each = col_stride // cols_axis
    row_groups = rows // row_stride
    col_groups = cols // col_stride
    group = row_groups * col_groups
    devices = rows_axis * cols_axis

    even_col, outer_cols, inner_cols = neighbours(frames[:, :, 0], frames[:, :, cols - 1], "wa")
    left = jnp.where(even_col, outer_cols, inner_cols)
    right = jnp.where(even_col, inner_cols, outer_cols)

    def edge(r):
        spare = jnp.zeros((frame_count, 14, channels), BF16)
        return jnp.concatenate([frames[:, r], left[:, r : r + 1], right[:, r : r + 1], spare], axis=1)

    even_row, outer_rows, inner_rows = neighbours(edge(0), edge(rows - 1), "ha")
    halo = (outer_rows, inner_rows, outer_cols, inner_cols)
    even = jnp.stack([even_row, even_col]).astype(jnp.int32)

    to_message = message_order(row_groups, cols, col_stride, cols_each)
    from_segments = np.kron(np.eye(row_groups), segment_order(cols, 1)).T
    order = jnp.asarray(to_message @ from_segments, BF16)
    order_back = jnp.asarray(to_message.T, BF16)
    def exchange(x):
        message = x.reshape(devices, -1, channels)
        return lax.all_to_all(message, ("ha", "wa"), split_axis=0, concat_axis=0, tiled=True).reshape(-1, channels)

    sent = []
    for f in range(frame_count):
        own, tokens = expand_call(f, frames, expand_weight)
        first = conv_call(
            f, keep, even, own, tokens, expand_weight, dw_kernel, conv_bias, order, halo, project_weight
        )
        sent.append(exchange(first))
    back = []
    for f in range(frame_count):
        x = sent[f]
        if group != 8:
            x = x.reshape(devices, cols_each, group, channels).swapaxes(0, 1).reshape(cols_each, -1, 8, channels)
            x = x.swapaxes(0, 1).reshape(-1, channels)
        x = window_call(f, keep, x, cols_each, 8, qkv_weight, out_weight, mlp_in, mlp_out)
        if group != 8:
            x = x.reshape(-1, cols_each, 8, channels).swapaxes(0, 1).reshape(cols_each, devices, group, channels)
            x = x.swapaxes(0, 1).reshape(-1, channels)
        back.append(exchange(x))
    result = None
    for f in range(frame_count):
        result = restore_call(f, back[f], order_back, frames.shape, result)
    return result


def solution(mesh):
    in_specs = (P(None, "ha", "wa", None), P(), P(), P(), P(), P(), P(), P(), P(), P())
    out_specs = P(None, "ha", "wa", None)
    return jax.shard_map(body, mesh=mesh, in_specs=in_specs, out_specs=out_specs, check_vma=False)
```

```python
import math

import jax
import jax.numpy as jnp
import numpy as np
from jax import lax
from jax.experimental import pallas as pl
from jax.experimental.pallas import tpu as pltpu
from jax.sharding import PartitionSpec as P

HEADS = 12
GRID = 16
SEG = 8
CHUNK = 1536
F32 = jnp.float32
BF16 = jnp.bfloat16
MIB = 1024 * 1024


def gelu(v):
    cubic = v * (math.sqrt(2 / math.pi) + (math.sqrt(2 / math.pi) * 0.044715) * (v * v))
    half = 0.5 * v
    return half + half * jnp.tanh(cubic)


def half_gelu(h):
    root = math.sqrt(2 / math.pi)
    return h + h * jnp.tanh(h * (2 * root + (8 * root * 0.044715) * (h * h)))


def normalize(values):
    mean_val = jnp.mean(values, axis=-1, keepdims=True)
    centred = values - mean_val
    variance = jnp.mean(centred * centred, axis=-1, keepdims=True)
    return centred * lax.rsqrt(variance + 1e-05)


def dot(a, b):
    return jnp.dot(a, b, preferred_element_type=F32)


def dot_t(a, b):
    return lax.dot_general(a, b, (((1,), (1,)), ((), ())), preferred_element_type=F32)


def segment_order(cols, count):
    steps = cols // SEG
    matrix = np.zeros((count * cols, count * cols), np.float32)
    for row in range(count):
        for t in range(steps):
            for s in range(SEG):
                matrix[row * cols + t * SEG + s, row * cols + s * steps + t] = 1
    return matrix


def segments(cols, count):
    steps = cols // SEG
    shape = (count * cols, count * cols)
    place = lax.broadcasted_iota(jnp.int32, shape, 0)
    inside = place % cols
    source = place - inside + inside % SEG * steps + inside // SEG
    return jnp.where(lax.broadcasted_iota(jnp.int32, shape, 1) == source, 0.5, 0.0).astype(BF16)


def message_order(row_groups, cols, col_stride, cols_each):
    col_groups = cols // col_stride
    dests = col_stride // cols_each
    matrix = np.zeros((row_groups * cols, row_groups * cols), np.float32)
    place = 0
    for w in range(dests):
        for b in range(cols_each):
            for g in range(row_groups):
                for h in range(col_groups):
                    matrix[place, g * cols + h * col_stride + w * cols_each + b] = 1
                    place += 1
    return matrix


def expand_kernel(frame, x_ref, expand_ref, expanded, tokens):
    rows, steps, _, hidden = expanded.shape
    cols = steps * SEG
    channels = x_ref.shape[-1]
    pair = 2 * cols
    seg = segments(cols, 2)
    for r in range(rows // 2):
        both = x_ref[frame, 2 * r : 2 * r + 2].reshape(pair, channels)
        tokens[r * pair : (r + 1) * pair] = dot(seg, both).astype(BF16)
    block = 4
    for c in range(hidden // CHUNK):
        lanes = slice(c * CHUNK, (c + 1) * CHUNK)
        for r in range(0, rows, block):
            value = half_gelu(dot(tokens[r * cols : (r + block) * cols], expand_ref[:, lanes]))
            expanded[r : r + block, :, :, lanes] = value.reshape(block, steps, SEG, CHUNK)


def expand_call(frame, x, expand_weight):
    _, rows, cols, channels = x.shape
    hidden = expand_weight.shape[1]

    def body(*refs):
        expand_kernel(frame, *refs)

    return pl.pallas_call(
        body,
        in_specs=[pl.BlockSpec(memory_space=pltpu.VMEM)] * 2,
        out_specs=[pl.BlockSpec(memory_space=pltpu.VMEM)] * 2,
        out_shape=[
            jax.ShapeDtypeStruct((rows, cols // SEG, SEG, hidden), F32),
            jax.ShapeDtypeStruct((rows * cols, channels), BF16),
        ],
        compiler_params=pltpu.CompilerParams(vmem_limit_bytes=24 * MIB),
        cost_estimate=pl.CostEstimate(flops=3 * 10**9, bytes_accessed=4 * 10**6, transcendentals=2 * 10**6),
    )(x, expand_weight)


def conv_kernel(
    frame,
    keep_ref,
    even_ref,
    own_ref,
    tokens,
    expand_ref,
    dw_any,
    bias_any,
    order_any,
    outer_rows_any,
    inner_rows_any,
    outer_cols_any,
    inner_cols_any,
    project_any,
    out_ref,
    dw_ref,
    bias_ref,
    order_ref,
    outer_rows,
    inner_rows,
    outer_cols,
    inner_cols,
    project_ref,
    sems,
    sides,
    side_vals,
    taps,
    edge_cols,
    edge_rows,
    mixed,
    total,
):
    rows, steps, _, hidden = own_ref.shape
    cols = steps * SEG
    pairs = [
        (outer_rows_any.at[frame], outer_rows),
        (inner_rows_any.at[frame], inner_rows),
        (outer_cols_any.at[frame], outer_cols),
        (inner_cols_any.at[frame], inner_cols),
        (dw_any, dw_ref),
        (bias_any, bias_ref),
        (project_any, project_ref),
        (order_any, order_ref),
    ]
    copies = [pltpu.make_async_copy(src, dst, sems.at[i]) for i, (src, dst) in enumerate(pairs)]
    for copy in copies:
        copy.start()
    sides[...] = jnp.zeros_like(sides)
    for copy in copies[0:4]:
        copy.wait()
    even_row, even_col = even_ref[0] == 1, even_ref[1] == 1
    outer, inner = outer_rows[...], inner_rows[...]
    top, bottom = jnp.where(even_row, outer, inner), jnp.where(even_row, inner, outer)
    outer, inner = outer_cols[...], inner_cols[...]
    left, right = jnp.where(even_col, outer, inner), jnp.where(even_col, inner, outer)
    seg_one = segments(cols, 1)
    top_tokens = dot(seg_one, top[0:cols]).astype(BF16)
    bottom_tokens = dot(seg_one, bottom[0:cols]).astype(BF16)
    top = 0.5 * top[cols : cols + 16].astype(F32)
    bottom = 0.5 * bottom[cols : cols + 16].astype(F32)
    sides[0:1] = top[0:1]
    sides[1 : rows + 1] = 0.5 * left.astype(F32)
    sides[rows + 1 : rows + 2] = bottom[0:1]
    sides[24:25] = top[1:2]
    sides[25 : rows + 25] = 0.5 * right.astype(F32)
    sides[rows + 25 : rows + 26] = bottom[1:2]
    halo = jnp.concatenate([top_tokens, bottom_tokens, sides[...].astype(BF16)], axis=0)
    place = lax.broadcasted_iota(jnp.int32, (SEG, CHUNK), 0)
    for copy in copies[4:6]:
        copy.wait()
    outside = 0.25 * (dw_ref[0] + dw_ref[2])
    centre = 0.25 * dw_ref[1]
    taps[0:3] = 0.5 * dw_ref[0]
    taps[3:6] = outside + centre
    taps[6:9] = outside - centre
    taps[9:12] = 0.5 * dw_ref[2]
    taps[12:13] = 0.5 * bias_ref[...].reshape(1, hidden)

    def expand_halo(c):
        lanes = slice(c * CHUNK, (c + 1) * CHUNK)
        value = half_gelu(dot(halo, expand_ref[:, lanes]))
        edge_rows[:, :, :, lanes] = value[: 2 * cols].reshape(2, steps, SEG, CHUNK)
        side_vals[:, lanes] = value[2 * cols :]

    def plain(r, t, lanes):
        if r == 0:
            return edge_rows[0, t, :, lanes]
        if r == rows + 1:
            return edge_rows[1, t, :, lanes]
        return own_ref[r - 1, t, :, lanes]

    def fill_edges(c, r):
        lanes = slice(c * CHUNK, (c + 1) * CHUNK)
        before = pltpu.roll(plain(r, steps - 1, lanes), 1, 0)
        edge_cols[r, 0, :, lanes] = jnp.where(place == 0, side_vals[r : r + 1, lanes], before)
        after = pltpu.roll(plain(r, 0, lanes), SEG - 1, 0)
        edge_cols[r, 1, :, lanes] = jnp.where(place == SEG - 1, side_vals[24 + r : 25 + r, lanes], after)

    def line(r, lanes):
        if r == 0:
            middle = edge_rows[0, :, :, lanes]
        elif r == rows + 1:
            middle = edge_rows[1, :, :, lanes]
        else:
            middle = own_ref[r - 1, :, :, lanes]
        return jnp.concatenate([edge_cols[r, 0:1, :, lanes], middle, edge_cols[r, 1:2, :, lanes]], axis=0)

    def conv_pair(c, r):
        upper, lower = [], []
        for lt in range(CHUNK // 128):
            lanes = slice(c * CHUNK + lt * 128, c * CHUNK + (lt + 1) * 128)
            d = [line(r + k, lanes) for k in range(4)]
            mixes = [d[0] - d[2], d[1] + d[2], d[2] - d[1], d[1] - d[3]]
            products = []
            for k in range(4):
                acc = jnp.broadcast_to(taps[12:13, lanes].reshape(1, 1, 128), (steps, SEG, 128)) if k == 1 else None
                for j in range(3):
                    term = mixes[k][j : j + steps] * taps[3 * k + j : 3 * k + j + 1, lanes].reshape(1, 1, 128)
                    acc = term if acc is None else acc + term
                products.append(acc)
            first = products[0] + products[1] + products[2]
            second = products[1] - products[2] - products[3]
            upper.append(half_gelu(first).reshape(cols, 128).astype(BF16))
            lower.append(half_gelu(second).reshape(cols, 128).astype(BF16))
        return jnp.concatenate([jnp.concatenate(upper, axis=1), jnp.concatenate(lower, axis=1)], axis=0)

    def project_rows(c, start, stop, values):
        lanes = slice(c * CHUNK, (c + 1) * CHUNK)
        span = slice(start * cols, stop * cols)
        branch = dot(jnp.concatenate(values, axis=0), project_ref[lanes])
        total[span] = branch if c == 0 else total[span] + branch

    part = rows // 2
    for c in range(hidden // CHUNK):
        expand_halo(c)
        if c == 0:
            copies[6].wait()
            copies[7].wait()
        fill_edges(c, 0)
        fill_edges(c, 1)
        values, ready = [], None
        for r in range(rows):
            fill_edges(c, r + 2)
            if r % 2 == 1:
                values.append(conv_pair(c, r - 1))
            if 2 * len(values) == part:
                if ready is not None:
                    project_rows(c, r + 1 - 2 * part, r + 1 - part, ready)
                ready, values = values, []
        project_rows(c, rows - part, rows, ready)

    flag = keep_ref[frame, 0].astype(F32)
    span = order_ref.shape[0]
    groups = span // cols
    stride = rows // groups
    order = order_ref[...]
    for d in range(stride):
        parts = []
        for g in range(groups):
            r = g * stride + d
            residual = 2.0 * tokens[r * cols : (r + 1) * cols].astype(F32)
            parts.append((residual + flag * total[r * cols : (r + 1) * cols]).astype(BF16))
        value = parts[0] if groups == 1 else jnp.concatenate(parts, axis=0)
        out_ref[d * span : (d + 1) * span] = dot(order, value).astype(BF16)


def conv_call(frame, keep, even, own, tokens, expand_weight, dw, bias, order, halo, project_weight):
    rows, steps, _, hidden = own.shape
    cols = steps * SEG
    channels = tokens.shape[1]
    large = [dw, bias, order, *halo, project_weight]

    def body(*refs):
        conv_kernel(frame, *refs)

    def buffer(a, k):
        return pltpu.VMEM(a.shape[1:] if 3 <= k < 7 else a.shape, a.dtype)

    return pl.pallas_call(
        body,
        in_specs=[pl.BlockSpec(memory_space=pltpu.SMEM)] * 2
        + [pl.BlockSpec(memory_space=pltpu.VMEM)] * 3
        + [pl.BlockSpec(memory_space=pl.ANY)] * len(large),
        out_specs=pl.BlockSpec(memory_space=pltpu.VMEM),
        out_shape=jax.ShapeDtypeStruct((rows * cols, channels), BF16),
        scratch_shapes=[buffer(a, k) for k, a in enumerate(large)]
        + [
            pltpu.SemaphoreType.DMA((len(large),)),
            pltpu.VMEM((48, channels), F32),
            pltpu.VMEM((48, hidden), F32),
            pltpu.VMEM((16, hidden), F32),
            pltpu.VMEM((rows + 2, 2, SEG, hidden), F32),
            pltpu.VMEM((2, steps, SEG, hidden), F32),
            pltpu.VMEM((rows * cols, hidden), BF16),
            pltpu.VMEM((rows * cols, channels), F32),
        ],
        compiler_params=pltpu.CompilerParams(vmem_limit_bytes=32 * MIB),
        cost_estimate=pl.CostEstimate(flops=4 * 10**9, bytes_accessed=4 * 10**6, transcendentals=2 * 10**6),
    )(keep, even, own, tokens, expand_weight, *large)


def window_kernel(frame, keep_ref, x_ref, qkv_ref, out_w_ref, in_ref, down_ref, out_ref, held):
    windows = held.shape[1]
    sources, _, group, channels = held.shape
    count = sources * group
    head_dim = channels // HEADS
    per_tile = 128 // head_dim
    scale = head_dim ** (-0.5) * math.log2(math.e)
    held[...] = x_ref[...].astype(F32).reshape(held.shape)
    attend_flag = keep_ref[frame, 1].astype(F32)
    mlp_flag = keep_ref[frame, 2].astype(F32)
    head_of_lane = lax.broadcasted_iota(jnp.int32, (1, 128), 1) // head_dim
    ones = jnp.ones((count, 128), BF16)
    none = jnp.zeros((), BF16)

    def attend(residual):
        qkv = dot(normalize(residual).astype(BF16), qkv_ref[...]).astype(BF16)
        tiles = []
        for t in range(channels // 128):
            queries = qkv[:, t * 128 : (t + 1) * 128]
            keys_part = qkv[:, channels + t * 128 : channels + (t + 1) * 128]
            values_part = qkv[:, 2 * channels + t * 128 : 2 * channels + (t + 1) * 128]
            values_part = jnp.concatenate([values_part, ones], axis=1)
            tile = None
            for i in range(per_tile):
                scores = dot_t(jnp.where(head_of_lane == i, queries, none), keys_part)
                top_score = jnp.max(scores, axis=1, keepdims=True)
                weights = jnp.exp2((scores - top_score) * scale).astype(BF16)
                both = dot(weights, values_part)
                share = both[:, :128] * (1.0 / both[:, 128:])
                tile = share if tile is None else jnp.where(head_of_lane == i, share, tile)
            tiles.append(tile.astype(BF16))
        update = dot(jnp.concatenate(tiles, axis=1), out_w_ref[...])
        return (residual + attend_flag * update).astype(BF16).astype(F32)

    def mlp(residual):
        inner = gelu(dot(normalize(residual).astype(BF16), in_ref[...])).astype(BF16)
        return residual + mlp_flag * dot(inner, down_ref[...])

    def one_window(w, _):
        second = attend(held[:, w].reshape(count, channels))
        held[:, w] = mlp(second).reshape(sources, group, channels)
        return 0

    lax.fori_loop(0, windows, one_window, 0)
    out_ref[...] = held[...].reshape(out_ref.shape).astype(BF16)


def window_call(frame, keep, x, windows, group, qkv_weight, out_weight, mlp_in, mlp_out):
    tokens, channels = x.shape
    held = (tokens // (windows * group), windows, group, channels)

    def body(*refs):
        window_kernel(frame, *refs)

    return pl.pallas_call(
        body,
        in_specs=[pl.BlockSpec(memory_space=pltpu.SMEM)] + [pl.BlockSpec(memory_space=pltpu.VMEM)] * 5,
        out_specs=pl.BlockSpec(memory_space=pltpu.VMEM),
        out_shape=jax.ShapeDtypeStruct(x.shape, BF16),
        scratch_shapes=[pltpu.VMEM(held, F32)],
        compiler_params=pltpu.CompilerParams(vmem_limit_bytes=40 * MIB),
        cost_estimate=pl.CostEstimate(flops=9 * 10**9, bytes_accessed=4 * 10**6, transcendentals=6 * 10**6),
    )(keep, x, qkv_weight, out_weight, mlp_in, mlp_out)


def restore_kernel(frame, x_ref, order_ref, *rest):
    out_any, rows_ref, sems = rest[-3:]
    rows, cols, channels = rows_ref.shape
    span = order_ref.shape[0]
    groups = span // cols
    stride = rows // groups
    order = order_ref[...]
    copies = []
    for d in range(stride):
        back = dot(order, x_ref[d * span : (d + 1) * span]).astype(BF16)
        for g in range(groups):
            r = g * stride + d
            rows_ref[r] = back[g * cols : (g + 1) * cols]
            copies.append(pltpu.make_async_copy(rows_ref.at[r], out_any.at[frame, r], sems.at[r]))
            copies[-1].start()
    for copy in copies:
        copy.wait()


def restore_call(frame, x, order, out_shape, previous):
    _, rows, cols, channels = out_shape

    def body(*refs):
        restore_kernel(frame, *refs)

    args = [x, order]
    specs = [pl.BlockSpec(memory_space=pltpu.VMEM)] * 2
    aliases = {}
    if previous is not None:
        aliases = {len(args): 0}
        args.append(previous)
        specs.append(pl.BlockSpec(memory_space=pl.ANY))
    return pl.pallas_call(
        body,
        in_specs=specs,
        out_specs=pl.BlockSpec(memory_space=pl.ANY),
        out_shape=jax.ShapeDtypeStruct(out_shape, BF16),
        scratch_shapes=[pltpu.VMEM((rows, cols, channels), BF16), pltpu.SemaphoreType.DMA((rows,))],
        input_output_aliases=aliases,
        compiler_params=pltpu.CompilerParams(vmem_limit_bytes=16 * MIB),
        cost_estimate=pl.CostEstimate(flops=10**8, bytes_accessed=2 * 10**6, transcendentals=0),
    )(*args)


def neighbours(first, last, axis):
    size = lax.axis_size(axis)
    even = lax.axis_index(axis) % 2 == 0
    inner = [(i, i ^ 1) for i in range(size)]
    outer = [(i, i + 1) for i in range(1, size - 1, 2)]
    outer = outer + [(j, i) for i, j in outer]
    across = lax.ppermute(jnp.where(even, first, last), axis, outer)
    within = lax.ppermute(jnp.where(even, last, first), axis, inner)
    return even, across, within


def body(
    frames,
    keep,
    expand_weight,
    dw_kernel,
    conv_bias,
    project_weight,
    qkv_weight,
    out_weight,
    mlp_in,
    mlp_out,
):
    frame_count, rows, cols, channels = frames.shape
    rows_axis = lax.axis_size("ha")
    cols_axis = lax.axis_size("wa")
    row_stride = rows * rows_axis // GRID
    col_stride = cols * cols_axis // GRID
    assert row_stride == rows_axis and col_stride % cols_axis == 0
    cols_each = col_stride // cols_axis
    row_groups = rows // row_stride
    col_groups = cols // col_stride
    group = row_groups * col_groups
    devices = rows_axis * cols_axis

    even_col, outer_cols, inner_cols = neighbours(frames[:, :, 0], frames[:, :, cols - 1], "wa")
    left = jnp.where(even_col, outer_cols, inner_cols)
    right = jnp.where(even_col, inner_cols, outer_cols)

    def edge(r):
        spare = jnp.zeros((frame_count, 14, channels), BF16)
        return jnp.concatenate([frames[:, r], left[:, r : r + 1], right[:, r : r + 1], spare], axis=1)

    even_row, outer_rows, inner_rows = neighbours(edge(0), edge(rows - 1), "ha")
    halo = (outer_rows, inner_rows, outer_cols, inner_cols)
    even = jnp.stack([even_row, even_col]).astype(jnp.int32)

    to_message = message_order(row_groups, cols, col_stride, cols_each)
    from_segments = np.kron(np.eye(row_groups), segment_order(cols, 1)).T
    order = jnp.asarray(to_message @ from_segments, BF16)
    order_back = jnp.asarray(to_message.T, BF16)
    def exchange(x):
        message = x.reshape(devices, -1, channels)
        return lax.all_to_all(message, ("ha", "wa"), split_axis=0, concat_axis=0, tiled=True).reshape(-1, channels)

    sent = []
    for f in range(frame_count):
        own, tokens = expand_call(f, frames, expand_weight)
        first = conv_call(
            f, keep, even, own, tokens, expand_weight, dw_kernel, conv_bias, order, halo, project_weight
        )
        sent.append(exchange(first))
    back = []
    for f in range(frame_count):
        x = sent[f]
        if group != 8:
            x = x.reshape(devices, cols_each, group, channels).swapaxes(0, 1).reshape(cols_each, -1, 8, channels)
            x = x.swapaxes(0, 1).reshape(-1, channels)
        x = window_call(f, keep, x, cols_each, 8, qkv_weight, out_weight, mlp_in, mlp_out)
        if group != 8:
            x = x.reshape(-1, cols_each, 8, channels).swapaxes(0, 1).reshape(cols_each, devices, group, channels)
            x = x.swapaxes(0, 1).reshape(-1, channels)
        back.append(exchange(x))
    result = None
    for f in range(frame_count):
        result = restore_call(f, back[f], order_back, frames.shape, result)
    return result


def solution(mesh):
    in_specs = (P(None, "ha", "wa", None), P(), P(), P(), P(), P(), P(), P(), P(), P())
    out_specs = P(None, "ha", "wa", None)
    return jax.shard_map(body, mesh=mesh, in_specs=in_specs, out_specs=out_specs, check_vma=False)
```

```python
import math

import jax
import jax.numpy as jnp
import numpy as np
from jax import lax
from jax.experimental import pallas as pl
from jax.experimental.pallas import tpu as pltpu
from jax.sharding import PartitionSpec as P

HEADS = 12
GRID = 16
SEG = 8
CHUNK = 1536
F32 = jnp.float32
BF16 = jnp.bfloat16
MIB = 1024 * 1024


def gelu(v):
    cubic = v * (math.sqrt(2 / math.pi) + (math.sqrt(2 / math.pi) * 0.044715) * (v * v))
    half = 0.5 * v
    return half + half * jnp.tanh(cubic)


def half_gelu(h):
    root = math.sqrt(2 / math.pi)
    return h + h * jnp.tanh(h * (2 * root + (8 * root * 0.044715) * (h * h)))


def normalize(values):
    mean_val = jnp.mean(values, axis=-1, keepdims=True)
    centred = values - mean_val
    variance = jnp.mean(centred * centred, axis=-1, keepdims=True)
    return centred * lax.rsqrt(variance + 1e-05)


def dot(a, b):
    return jnp.dot(a, b, preferred_element_type=F32)


def dot_t(a, b):
    return lax.dot_general(a, b, (((1,), (1,)), ((), ())), preferred_element_type=F32)


def segment_order(cols, count):
    steps = cols // SEG
    matrix = np.zeros((count * cols, count * cols), np.float32)
    for row in range(count):
        for t in range(steps):
            for s in range(SEG):
                matrix[row * cols + t * SEG + s, row * cols + s * steps + t] = 1
    return matrix


def segments(cols, count):
    steps = cols // SEG
    shape = (count * cols, count * cols)
    place = lax.broadcasted_iota(jnp.int32, shape, 0)
    inside = place % cols
    source = place - inside + inside % SEG * steps + inside // SEG
    return jnp.where(lax.broadcasted_iota(jnp.int32, shape, 1) == source, 0.5, 0.0).astype(BF16)


def message_order(row_groups, cols, col_stride, cols_each):
    col_groups = cols // col_stride
    dests = col_stride // cols_each
    matrix = np.zeros((row_groups * cols, row_groups * cols), np.float32)
    place = 0
    for w in range(dests):
        for b in range(cols_each):
            for g in range(row_groups):
                for h in range(col_groups):
                    matrix[place, g * cols + h * col_stride + w * cols_each + b] = 1
                    place += 1
    return matrix


def expand_kernel(frame, x_ref, expand_ref, expanded, tokens):
    rows, steps, _, hidden = expanded.shape
    cols = steps * SEG
    channels = x_ref.shape[-1]
    pair = 2 * cols
    seg = segments(cols, 2)
    for r in range(rows // 2):
        both = x_ref[frame, 2 * r : 2 * r + 2].reshape(pair, channels)
        tokens[r * pair : (r + 1) * pair] = dot(seg, both).astype(BF16)
    block = 4
    for c in range(hidden // CHUNK):
        lanes = slice(c * CHUNK, (c + 1) * CHUNK)
        for r in range(0, rows, block):
            value = half_gelu(dot(tokens[r * cols : (r + block) * cols], expand_ref[:, lanes]))
            expanded[r : r + block, :, :, lanes] = value.reshape(block, steps, SEG, CHUNK)


def expand_call(frame, x, expand_weight):
    _, rows, cols, channels = x.shape
    hidden = expand_weight.shape[1]

    def body(*refs):
        expand_kernel(frame, *refs)

    return pl.pallas_call(
        body,
        in_specs=[pl.BlockSpec(memory_space=pltpu.VMEM)] * 2,
        out_specs=[pl.BlockSpec(memory_space=pltpu.VMEM)] * 2,
        out_shape=[
            jax.ShapeDtypeStruct((rows, cols // SEG, SEG, hidden), F32),
            jax.ShapeDtypeStruct((rows * cols, channels), BF16),
        ],
        compiler_params=pltpu.CompilerParams(vmem_limit_bytes=24 * MIB),
        cost_estimate=pl.CostEstimate(flops=3 * 10**9, bytes_accessed=4 * 10**6, transcendentals=2 * 10**6),
    )(x, expand_weight)


def conv_kernel(
    frame,
    keep_ref,
    even_ref,
    own_ref,
    tokens,
    expand_ref,
    dw_any,
    bias_any,
    order_any,
    outer_rows_any,
    inner_rows_any,
    outer_cols_any,
    inner_cols_any,
    project_any,
    out_ref,
    dw_ref,
    bias_ref,
    order_ref,
    outer_rows,
    inner_rows,
    outer_cols,
    inner_cols,
    project_ref,
    sems,
    sides,
    side_vals,
    taps,
    edge_cols,
    edge_rows,
    mixed,
    total,
):
    rows, steps, _, hidden = own_ref.shape
    cols = steps * SEG
    pairs = [
        (outer_rows_any.at[frame], outer_rows),
        (inner_rows_any.at[frame], inner_rows),
        (outer_cols_any.at[frame], outer_cols),
        (inner_cols_any.at[frame], inner_cols),
        (dw_any, dw_ref),
        (bias_any, bias_ref),
        (project_any, project_ref),
        (order_any, order_ref),
    ]
    copies = [pltpu.make_async_copy(src, dst, sems.at[i]) for i, (src, dst) in enumerate(pairs)]
    for copy in copies:
        copy.start()
    sides[...] = jnp.zeros_like(sides)
    for copy in copies[0:4]:
        copy.wait()
    even_row, even_col = even_ref[0] == 1, even_ref[1] == 1
    outer, inner = outer_rows[...], inner_rows[...]
    top, bottom = jnp.where(even_row, outer, inner), jnp.where(even_row, inner, outer)
    outer, inner = outer_cols[...], inner_cols[...]
    left, right = jnp.where(even_col, outer, inner), jnp.where(even_col, inner, outer)
    seg_one = segments(cols, 1)
    top_tokens = dot(seg_one, top[0:cols]).astype(BF16)
    bottom_tokens = dot(seg_one, bottom[0:cols]).astype(BF16)
    top = 0.5 * top[cols : cols + 16].astype(F32)
    bottom = 0.5 * bottom[cols : cols + 16].astype(F32)
    sides[0:1] = top[0:1]
    sides[1 : rows + 1] = 0.5 * left.astype(F32)
    sides[rows + 1 : rows + 2] = bottom[0:1]
    sides[24:25] = top[1:2]
    sides[25 : rows + 25] = 0.5 * right.astype(F32)
    sides[rows + 25 : rows + 26] = bottom[1:2]
    halo = jnp.concatenate([top_tokens, bottom_tokens, sides[...].astype(BF16)], axis=0)
    place = lax.broadcasted_iota(jnp.int32, (SEG, CHUNK), 0)
    for copy in copies[4:6]:
        copy.wait()
    outside = 0.25 * (dw_ref[0] + dw_ref[2])
    centre = 0.25 * dw_ref[1]
    taps[0:3] = 0.5 * dw_ref[0]
    taps[3:6] = outside + centre
    taps[6:9] = outside - centre
    taps[9:12] = 0.5 * dw_ref[2]
    taps[12:13] = 0.5 * bias_ref[...].reshape(1, hidden)

    def expand_halo(c):
        lanes = slice(c * CHUNK, (c + 1) * CHUNK)
        value = half_gelu(dot(halo, expand_ref[:, lanes]))
        edge_rows[:, :, :, lanes] = value[: 2 * cols].reshape(2, steps, SEG, CHUNK)
        side_vals[:, lanes] = value[2 * cols :]

    def plain(r, t, lanes):
        if r == 0:
            return edge_rows[0, t, :, lanes]
        if r == rows + 1:
            return edge_rows[1, t, :, lanes]
        return own_ref[r - 1, t, :, lanes]

    def fill_edges(c, r):
        lanes = slice(c * CHUNK, (c + 1) * CHUNK)
        before = pltpu.roll(plain(r, steps - 1, lanes), 1, 0)
        edge_cols[r, 0, :, lanes] = jnp.where(place == 0, side_vals[r : r + 1, lanes], before)
        after = pltpu.roll(plain(r, 0, lanes), SEG - 1, 0)
        edge_cols[r, 1, :, lanes] = jnp.where(place == SEG - 1, side_vals[24 + r : 25 + r, lanes], after)

    def line(r, lanes):
        if r == 0:
            middle = edge_rows[0, :, :, lanes]
        elif r == rows + 1:
            middle = edge_rows[1, :, :, lanes]
        else:
            middle = own_ref[r - 1, :, :, lanes]
        return jnp.concatenate([edge_cols[r, 0:1, :, lanes], middle, edge_cols[r, 1:2, :, lanes]], axis=0)

    def conv_pair(c, r):
        upper, lower = [], []
        for lt in range(CHUNK // 128):
            lanes = slice(c * CHUNK + lt * 128, c * CHUNK + (lt + 1) * 128)
            d = [line(r + k, lanes) for k in range(4)]
            mixes = [d[0] - d[2], d[1] + d[2], d[2] - d[1], d[1] - d[3]]
            products = []
            for k in range(4):
                acc = jnp.broadcast_to(taps[12:13, lanes].reshape(1, 1, 128), (steps, SEG, 128)) if k == 1 else None
                for j in range(3):
                    term = mixes[k][j : j + steps] * taps[3 * k + j : 3 * k + j + 1, lanes].reshape(1, 1, 128)
                    acc = term if acc is None else acc + term
                products.append(acc)
            first = products[0] + products[1] + products[2]
            second = products[1] - products[2] - products[3]
            upper.append(half_gelu(first).reshape(cols, 128).astype(BF16))
            lower.append(half_gelu(second).reshape(cols, 128).astype(BF16))
        return jnp.concatenate([jnp.concatenate(upper, axis=1), jnp.concatenate(lower, axis=1)], axis=0)

    def project_rows(c, start, stop, values):
        lanes = slice(c * CHUNK, (c + 1) * CHUNK)
        span = slice(start * cols, stop * cols)
        branch = dot(jnp.concatenate(values, axis=0), project_ref[lanes])
        total[span] = branch if c == 0 else total[span] + branch

    part = rows
    for c in range(hidden // CHUNK):
        expand_halo(c)
        if c == 0:
            copies[6].wait()
            copies[7].wait()
        fill_edges(c, 0)
        fill_edges(c, 1)
        values, ready = [], None
        for r in range(rows):
            fill_edges(c, r + 2)
            if r % 2 == 1:
                values.append(conv_pair(c, r - 1))
            if 2 * len(values) == part:
                if ready is not None:
                    project_rows(c, r + 1 - 2 * part, r + 1 - part, ready)
                ready, values = values, []
        project_rows(c, rows - part, rows, ready)

    flag = keep_ref[frame, 0].astype(F32)
    span = order_ref.shape[0]
    groups = span // cols
    stride = rows // groups
    order = order_ref[...]
    for d in range(stride):
        parts = []
        for g in range(groups):
            r = g * stride + d
            residual = 2.0 * tokens[r * cols : (r + 1) * cols].astype(F32)
            parts.append((residual + flag * total[r * cols : (r + 1) * cols]).astype(BF16))
        value = parts[0] if groups == 1 else jnp.concatenate(parts, axis=0)
        out_ref[d * span : (d + 1) * span] = dot(order, value).astype(BF16)


def conv_call(frame, keep, even, own, tokens, expand_weight, dw, bias, order, halo, project_weight):
    rows, steps, _, hidden = own.shape
    cols = steps * SEG
    channels = tokens.shape[1]
    large = [dw, bias, order, *halo, project_weight]

    def body(*refs):
        conv_kernel(frame, *refs)

    def buffer(a, k):
        return pltpu.VMEM(a.shape[1:] if 3 <= k < 7 else a.shape, a.dtype)

    return pl.pallas_call(
        body,
        in_specs=[pl.BlockSpec(memory_space=pltpu.SMEM)] * 2
        + [pl.BlockSpec(memory_space=pltpu.VMEM)] * 3
        + [pl.BlockSpec(memory_space=pl.ANY)] * len(large),
        out_specs=pl.BlockSpec(memory_space=pltpu.VMEM),
        out_shape=jax.ShapeDtypeStruct((rows * cols, channels), BF16),
        scratch_shapes=[buffer(a, k) for k, a in enumerate(large)]
        + [
            pltpu.SemaphoreType.DMA((len(large),)),
            pltpu.VMEM((48, channels), F32),
            pltpu.VMEM((48, hidden), F32),
            pltpu.VMEM((16, hidden), F32),
            pltpu.VMEM((rows + 2, 2, SEG, hidden), F32),
            pltpu.VMEM((2, steps, SEG, hidden), F32),
            pltpu.VMEM((rows * cols, hidden), BF16),
            pltpu.VMEM((rows * cols, channels), F32),
        ],
        compiler_params=pltpu.CompilerParams(vmem_limit_bytes=32 * MIB),
        cost_estimate=pl.CostEstimate(flops=4 * 10**9, bytes_accessed=4 * 10**6, transcendentals=2 * 10**6),
    )(keep, even, own, tokens, expand_weight, *large)


def window_kernel(frame, keep_ref, x_ref, qkv_ref, out_w_ref, in_ref, down_ref, out_ref, held):
    windows = held.shape[1]
    sources, _, group, channels = held.shape
    count = sources * group
    head_dim = channels // HEADS
    per_tile = 128 // head_dim
    scale = head_dim ** (-0.5) * math.log2(math.e)
    held[...] = x_ref[...].astype(F32).reshape(held.shape)
    attend_flag = keep_ref[frame, 1].astype(F32)
    mlp_flag = keep_ref[frame, 2].astype(F32)
    head_of_lane = lax.broadcasted_iota(jnp.int32, (1, 128), 1) // head_dim
    ones = jnp.ones((count, 128), BF16)
    none = jnp.zeros((), BF16)

    def attend(residual):
        qkv = dot(normalize(residual).astype(BF16), qkv_ref[...]).astype(BF16)
        tiles = []
        for t in range(channels // 128):
            queries = qkv[:, t * 128 : (t + 1) * 128]
            keys_part = qkv[:, channels + t * 128 : channels + (t + 1) * 128]
            values_part = qkv[:, 2 * channels + t * 128 : 2 * channels + (t + 1) * 128]
            values_part = jnp.concatenate([values_part, ones], axis=1)
            tile = None
            for i in range(per_tile):
                scores = dot_t(jnp.where(head_of_lane == i, queries, none), keys_part)
                top_score = jnp.max(scores, axis=1, keepdims=True)
                weights = jnp.exp2((scores - top_score) * scale).astype(BF16)
                both = dot(weights, values_part)
                share = both[:, :128] * (1.0 / both[:, 128:])
                tile = share if tile is None else jnp.where(head_of_lane == i, share, tile)
            tiles.append(tile.astype(BF16))
        update = dot(jnp.concatenate(tiles, axis=1), out_w_ref[...])
        return (residual + attend_flag * update).astype(BF16).astype(F32)

    def mlp(residual):
        inner = gelu(dot(normalize(residual).astype(BF16), in_ref[...])).astype(BF16)
        return residual + mlp_flag * dot(inner, down_ref[...])

    def one_window(w, _):
        second = attend(held[:, w].reshape(count, channels))
        held[:, w] = mlp(second).reshape(sources, group, channels)
        return 0

    lax.fori_loop(0, windows, one_window, 0)
    out_ref[...] = held[...].reshape(out_ref.shape).astype(BF16)


def window_call(frame, keep, x, windows, group, qkv_weight, out_weight, mlp_in, mlp_out):
    tokens, channels = x.shape
    held = (tokens // (windows * group), windows, group, channels)

    def body(*refs):
        window_kernel(frame, *refs)

    return pl.pallas_call(
        body,
        in_specs=[pl.BlockSpec(memory_space=pltpu.SMEM)] + [pl.BlockSpec(memory_space=pltpu.VMEM)] * 5,
        out_specs=pl.BlockSpec(memory_space=pltpu.VMEM),
        out_shape=jax.ShapeDtypeStruct(x.shape, BF16),
        scratch_shapes=[pltpu.VMEM(held, F32)],
        compiler_params=pltpu.CompilerParams(vmem_limit_bytes=40 * MIB),
        cost_estimate=pl.CostEstimate(flops=9 * 10**9, bytes_accessed=4 * 10**6, transcendentals=6 * 10**6),
    )(keep, x, qkv_weight, out_weight, mlp_in, mlp_out)


def restore_kernel(x_ref, order_ref, *rest):
    out_ref = rest[-1]
    _, rows, cols, channels = out_ref.shape
    span = order_ref.shape[0]
    groups = span // cols
    stride = rows // groups
    order = order_ref[...]
    for d in range(stride):
        back = dot(order, x_ref[d * span : (d + 1) * span]).astype(BF16)
        for g in range(groups):
            out_ref[0, g * stride + d] = back[g * cols : (g + 1) * cols]


def restore_call(frame, x, order, out_shape, previous):
    _, rows, cols, channels = out_shape

    def whole(a):
        return pl.BlockSpec(a.shape, lambda i, n=a.ndim: (0,) * n)

    args = [x, order]
    specs = [whole(a) for a in args]
    aliases = {}
    if previous is not None:
        aliases = {len(args): 0}
        args.append(previous)
        specs.append(pl.BlockSpec(memory_space=pl.ANY))
    return pl.pallas_call(
        restore_kernel,
        grid=(1,),
        in_specs=specs,
        out_specs=pl.BlockSpec((1, rows, cols, channels), lambda i: (frame, 0, 0, 0)),
        out_shape=jax.ShapeDtypeStruct(out_shape, BF16),
        input_output_aliases=aliases,
        compiler_params=pltpu.CompilerParams(vmem_limit_bytes=16 * MIB),
        cost_estimate=pl.CostEstimate(flops=10**8, bytes_accessed=2 * 10**6, transcendentals=0),
    )(*args)


def neighbours(first, last, axis):
    size = lax.axis_size(axis)
    even = lax.axis_index(axis) % 2 == 0
    inner = [(i, i ^ 1) for i in range(size)]
    outer = [(i, i + 1) for i in range(1, size - 1, 2)]
    outer = outer + [(j, i) for i, j in outer]
    across = lax.ppermute(jnp.where(even, first, last), axis, outer)
    within = lax.ppermute(jnp.where(even, last, first), axis, inner)
    return even, across, within


def body(
    frames,
    keep,
    expand_weight,
    dw_kernel,
    conv_bias,
    project_weight,
    qkv_weight,
    out_weight,
    mlp_in,
    mlp_out,
):
    frame_count, rows, cols, channels = frames.shape
    rows_axis = lax.axis_size("ha")
    cols_axis = lax.axis_size("wa")
    row_stride = rows * rows_axis // GRID
    col_stride = cols * cols_axis // GRID
    assert row_stride == rows_axis and col_stride % cols_axis == 0
    cols_each = col_stride // cols_axis
    row_groups = rows // row_stride
    col_groups = cols // col_stride
    group = row_groups * col_groups
    devices = rows_axis * cols_axis

    even_col, outer_cols, inner_cols = neighbours(frames[:, :, 0], frames[:, :, cols - 1], "wa")
    left = jnp.where(even_col, outer_cols, inner_cols)
    right = jnp.where(even_col, inner_cols, outer_cols)

    def edge(r):
        spare = jnp.zeros((frame_count, 14, channels), BF16)
        return jnp.concatenate([frames[:, r], left[:, r : r + 1], right[:, r : r + 1], spare], axis=1)

    even_row, outer_rows, inner_rows = neighbours(edge(0), edge(rows - 1), "ha")
    halo = (outer_rows, inner_rows, outer_cols, inner_cols)
    even = jnp.stack([even_row, even_col]).astype(jnp.int32)

    to_message = message_order(row_groups, cols, col_stride, cols_each)
    from_segments = np.kron(np.eye(row_groups), segment_order(cols, 1)).T
    order = jnp.asarray(to_message @ from_segments, BF16)
    order_back = jnp.asarray(to_message.T, BF16)
    def exchange(x):
        message = x.reshape(devices, -1, channels)
        return lax.all_to_all(message, ("ha", "wa"), split_axis=0, concat_axis=0, tiled=True).reshape(-1, channels)

    sent = []
    for f in range(frame_count):
        own, tokens = expand_call(f, frames, expand_weight)
        first = conv_call(
            f, keep, even, own, tokens, expand_weight, dw_kernel, conv_bias, order, halo, project_weight
        )
        sent.append(exchange(first))
    back = []
    for f in range(frame_count):
        x = sent[f]
        if group != 8:
            x = x.reshape(devices, cols_each, group, channels).swapaxes(0, 1).reshape(cols_each, -1, 8, channels)
            x = x.swapaxes(0, 1).reshape(-1, channels)
        x = window_call(f, keep, x, cols_each, 8, qkv_weight, out_weight, mlp_in, mlp_out)
        if group != 8:
            x = x.reshape(-1, cols_each, 8, channels).swapaxes(0, 1).reshape(cols_each, devices, group, channels)
            x = x.swapaxes(0, 1).reshape(-1, channels)
        back.append(exchange(x))
    result = None
    for f in range(frame_count):
        result = restore_call(f, back[f], order_back, frames.shape, result)
    return result


def solution(mesh):
    in_specs = (P(None, "ha", "wa", None), P(), P(), P(), P(), P(), P(), P(), P(), P())
    out_specs = P(None, "ha", "wa", None)
    return jax.shard_map(body, mesh=mesh, in_specs=in_specs, out_specs=out_specs, check_vma=False)
```
